512 devices in a mesh: ctx: 128 (over y, z, core), kvh: 4 (over x).
Axes of the slice: x: 4, y: 8, z: 8, core: 2. Of those that a mesh axis runs over, the one named last changes fastest.
Arguments:
- hidden: bfloat16 [3, 4, 4096], P(None, None, 'ctx'), may hold values from -6 to 6
- w_query: bfloat16 [4096, 8192], P('ctx', 'kvh'), may hold values from -0.09375 to 0.09375
- q_gain: float32 [128], replicated, may hold values from 0.25 to 1.75
- basis: float32 [4, 128, 128], P('kvh'), may hold values from -0.5 to 0.5
- keys: bfloat16 [4, 4, 196608, 128], P(None, 'kvh', 'ctx'), may hold values from -2500 to 2500
- values: bfloat16 [4, 4, 196608, 128], P(None, 'kvh', 'ctx'), may hold values from -6 to 6
- new_keys: bfloat16 [3, 4, 4, 128], P(None, None, 'kvh'), may hold values from -25 to 25
- new_values: bfloat16 [3, 4, 4, 128], P(None, None, 'kvh'), may hold values from -6 to 6
- block_lists: int32 [3, 4, 4, 256], P(None, None, 'kvh'), may hold values from 0 to 1535, as said below
- w_out: bfloat16 [8192, 4096], P('kvh', 'ctx'), may hold values from -0.5 to 0.5
Outputs:
- block_logmass: float32 [3, 4, 64, 1536], P(None, None, 'kvh', 'ctx')
- layer_out: bfloat16 [3, 4, 4096], P(None, None, 'ctx')
The draws below stay inside these ranges and needn't reach their ends.
Inputs may be any that keep to these rules, and one draw needn't show every extreme that they name: `block_lists`: each list holds 256 distinct block numbers in ascending order. Counted per index of ctx (blocks i * 12 to i * 12 + 11), a list has at most 8 of them there, and in every list some index holds exactly 8.
All inputs are finite; a program needn't handle non-finite values.
Results may differ from the reference program's by a relative error of at most 0.017.
Values may be sent and summed in bfloat16 or wider, within the bound.
A program may use at most 128 MiB of HBM per device.

```python
import jax
import jax.numpy as jnp
from jax import lax

HID = 4096
HQ = 64
KVH = 4
HD = 128
RANK = 32
BLK = 128
STEPS = 3
REQ = 4
MOST = 8
HG = 16
LB = 12
CTX = 196608
NB = 1536
KSEL = 256


def draw_keys(key, part):
    key = jax.random.fold_in(key, 11)
    key_one = jax.random.fold_in(key, 0)
    shape = (REQ, KVH, CTX, HD)
    base = 3.0 * jax.random.truncated_normal(key_one, -4.0, 4.0, shape, jnp.float32)
    return base.astype(jnp.bfloat16)


def draw_block_lists(key, part):
    key = jax.random.fold_in(key, 23)
    key_one, key_two, key_three = jax.random.split(key, 3)
    n_lists = STEPS * REQ * KVH
    n_groups = NB // LB // 4
    n_shards = NB // LB
    cuts = jnp.sort(jax.random.randint(key_one, (n_lists, n_groups, 3), 0, MOST + 1), axis=-1)
    edges = jnp.concatenate([jnp.zeros((n_lists, n_groups, 1), jnp.int32), cuts, jnp.full((n_lists, n_groups, 1), MOST, jnp.int32)], axis=-1)
    counts = edges[..., 1:] - edges[..., :-1]
    counts = counts.at[:, 0, :].set(jnp.array([MOST, 0, 0, 0], jnp.int32))
    counts = counts.reshape(n_lists, n_shards)
    orders = jax.vmap(lambda one_key: jax.random.permutation(one_key, n_shards))(jax.random.split(key_two, n_lists))
    counts = jnp.take_along_axis(counts, orders, axis=1)
    scores = jax.random.randint(key_three, (n_lists, n_shards, LB), 0, 4 * LB) * LB + jnp.arange(LB, dtype=jnp.int32)
    ranks = jnp.argsort(jnp.argsort(scores, axis=-1), axis=-1)
    chosen = (ranks < counts[..., None]).reshape(n_lists, NB).astype(jnp.int32)
    picked = jnp.argsort(1 - chosen, axis=-1, stable=True)[:, :KSEL]
    return picked.astype(jnp.int32).reshape(STEPS, REQ, KVH, KSEL)


def block_scale(stream_key, dims, pieces, low, high):
    def one(dim, parts):
        draws = jax.random.uniform(jax.random.fold_in(jax.random.fold_in(stream_key, 6), dim), (parts,), jnp.float32, low / len(pieces), high / len(pieces))
        return jnp.repeat(jnp.exp(draws), dims[dim] // parts).reshape((-1,) + (1,) * (len(dims) - dim - 1))

    gain = one(*pieces[0])
    for cut in pieces[1:]:
        gain = gain * one(*cut)
    return gain


def normal_values(rng, shape, spread, limit, shards=(), kind=jnp.bfloat16):
    values = spread * jax.random.normal(rng, shape, jnp.float32)
    if shards:
        values = values * block_scale(rng, shape, shards, -0.22, 0.18)
    return jnp.clip(values, -limit, limit).astype(kind)


def setup_inputs(seed: int = 0) -> dict:
    key_list = jax.random.split(jax.random.key(seed), 11)
    hidden = normal_values(key_list[0], (STEPS, REQ, HID), 1.0, 6.0, ((2, 128),))
    w_query = normal_values(key_list[1], (HID, HQ * HD), HID ** -0.5, 0.09375, ((0, 128), (1, 4)))
    q_gain = jnp.clip(1.0 + 0.15 * jax.random.normal(key_list[2], (HD,), jnp.float32), 0.25, 1.75)
    basis = normal_values(key_list[3], (KVH, HD, HD), HD ** -0.5, 0.5, ((0, 4),), jnp.float32)
    keys = draw_keys(jax.random.fold_in(key_list[10], 71), 0)
    values = normal_values(key_list[5], (REQ, KVH, CTX, HD), 1.0, 6.0, ((1, 4), (2, 128)))
    new_keys = normal_values(key_list[6], (STEPS, REQ, KVH, HD), 5.0, 25.0, ((2, 4),))
    new_values = normal_values(key_list[7], (STEPS, REQ, KVH, HD), 1.0, 6.0, ((2, 4),))
    block_lists = draw_block_lists(jax.random.fold_in(key_list[10], 71), 0)
    w_out = normal_values(key_list[9], (HQ * HD, HID), HD ** -0.5, 0.5, ((0, 4), (1, 128)))
    return {"hidden": hidden, "w_query": w_query, "q_gain": q_gain, "basis": basis, "keys": keys, "values": values, "new_keys": new_keys, "new_values": new_values, "block_lists": block_lists, "w_out": w_out}


def log_sum_exp(scores, axis, keepdims=False):
    peak = lax.optimization_barrier(jnp.max(scores, axis=axis, keepdims=True))
    summed = jnp.log(lax.optimization_barrier(jnp.sum(jnp.exp(scores - peak), axis=axis, keepdims=True))) + peak
    if keepdims:
        return summed
    return jnp.squeeze(summed, axis=axis)

def pair_terms(pair, q_rot, keys, values, new_keys, new_values, block_lists):
    req_id = pair // KVH
    head_id = pair % KVH
    key_all = keys[req_id, head_id].astype(jnp.float32)
    val_all = values[req_id, head_id]
    query_rows = q_rot[:, req_id, head_id]
    scale = 1.0 / HD ** 0.5
    low_score = jnp.einsum('sgc,tc->sgt', query_rows[..., :RANK], key_all[:, :RANK], precision=lax.Precision.HIGHEST) * scale
    block_lse = log_sum_exp(low_score.reshape(STEPS, HG, NB, BLK), -1)
    total_lse = log_sum_exp(block_lse, -1, True)
    logmass = block_lse - total_lse
    fresh_keys = new_keys[:, req_id, head_id].astype(jnp.float32)
    fresh_vals = new_values[:, req_id, head_id]
    outputs = []
    for step_no in range(STEPS):
        block_ids = block_lists[step_no, req_id, head_id].astype(jnp.int32)
        tok_ids = (block_ids[:, None] * BLK + jnp.arange(BLK, dtype=jnp.int32)[None, :]).reshape(-1)
        sel_keys = key_all[tok_ids]
        sel_vals = val_all[tok_ids]
        exact = jnp.dot(query_rows[step_no], sel_keys.T, precision=lax.Precision.HIGHEST) * scale
        fresh = jnp.dot(query_rows[step_no], fresh_keys.T, precision=lax.Precision.HIGHEST) * scale
        seen = jnp.arange(STEPS) <= step_no
        fresh = jnp.where(seen[None, :], fresh, -1e+30)
        top = jnp.maximum(lax.optimization_barrier(jnp.max(exact, axis=-1)), lax.optimization_barrier(jnp.max(fresh, axis=-1)))[:, None]
        old_w = jnp.exp(exact - top)
        new_w = jnp.where(seen[None, :], jnp.exp(fresh - top), 0.0)
        total = lax.optimization_barrier(jnp.sum(old_w, axis=-1)) + lax.optimization_barrier(jnp.sum(new_w, axis=-1))
        acc = jnp.dot(old_w.astype(jnp.bfloat16), sel_vals, preferred_element_type=jnp.float32)
        acc = acc + jnp.dot(new_w.astype(jnp.bfloat16), fresh_vals, preferred_element_type=jnp.float32)
        outputs.append((acc / total[:, None]).astype(jnp.bfloat16))
    return (logmass, jnp.stack(outputs))

def reference(hidden, w_query, q_gain, basis, keys, values, new_keys, new_values, block_lists, w_out):
    query = jnp.dot(hidden.reshape(STEPS * REQ, HID), w_query, preferred_element_type=jnp.float32)
    query = query.reshape(STEPS, REQ, HQ, HD)
    normed = query * lax.rsqrt(lax.optimization_barrier(jnp.mean(query * query, axis=-1, keepdims=True)) + 1e-06) * q_gain
    grouped = normed.reshape(STEPS, REQ, KVH, HG, HD)
    q_rot = jnp.einsum('srkgd,kde->srkge', grouped, basis.astype(jnp.float32), precision=lax.Precision.HIGHEST)

    def one_pair(pair):
        return pair_terms(pair, q_rot, keys, values, new_keys, new_values, block_lists)
    logmass, attn = lax.map(one_pair, jnp.arange(REQ * KVH, dtype=jnp.int32))
    logmass = logmass.reshape(REQ, KVH, STEPS, HG, NB).transpose(2, 0, 1, 3, 4).reshape(STEPS, REQ, HQ, NB)
    attn = attn.reshape(REQ, KVH, STEPS, HG, HD).transpose(2, 0, 1, 3, 4).reshape(STEPS * REQ, KVH, HG * HD)
    w_groups = w_out.reshape(KVH, HG * HD, HID)
    group_out = jnp.einsum('nkf,kfh->knh', attn.astype(jnp.float32), w_groups.astype(jnp.float32), precision=lax.Precision.HIGHEST).astype(jnp.bfloat16)
    layer_out = lax.optimization_barrier(jnp.sum(group_out.astype(jnp.float32), axis=0)).astype(jnp.bfloat16)
    return (logmass, layer_out.reshape(STEPS, REQ, HID))
```

```python
import jax
import jax.numpy as jnp
from jax import lax
from jax.experimental import pallas as pl
from jax.experimental.pallas import tpu as pltpu
from jax.sharding import PartitionSpec as P

RANK = 32
BLK = 128
STEPS = 3
REQ = 4
ROWS = STEPS * REQ
SLOT = 16
STAT = 12
LOW = 16
HEADS = 16
HALF = 8
HD = 128
NONE = -1e30
MESH = pl.DeviceIdType.MESH
F32 = jnp.float32
BF16 = jnp.bfloat16


def split3(x):
    hi = x.astype(BF16)
    rest = x - hi.astype(F32)
    mid = rest.astype(BF16)
    lo = (rest - mid.astype(F32)).astype(BF16)
    return hi, mid, lo


def slot(i):
    if isinstance(i, int):
        return pl.ds(i * SLOT, SLOT)
    return pl.ds(pl.multiple_of(i * SLOT, SLOT), SLOT)


def iota(shape, dim):
    return lax.broadcasted_iota(jnp.int32, shape, dim)


def column(row):
    diag = iota((SLOT, HD), 0) == iota((SLOT, HD), 1)
    return jnp.sum(jnp.where(diag, row, 0.0), axis=1, keepdims=True)


def kernel(
    hid_h, wq_h, gain_h, basis_h, keys_h, vals_h, nk_h, nv_h, lists_h, wo_h,
    mass_o, out_o,
    hid_v, wq_v, gain_v, basis_v, keys_v, vals_v, nk_v, nv_v, lists_v, wo_v,
    list_rows, bias, nk_rows, nv_rows, rot,
    q_part, q_core, q_half, q_rs, q_own, q_ex, q_all,
    o_part, o_core, o_half, o_rs, o_own, o_ex, o_all, lse_all,
    x_own, x_in,
    in_sem, core_s, core_r, rs_s, rs_r, ex_s, ex_r, ag_s, ag_r, x_s, x_r,
):
    ctx = lax.axis_index("ctx")
    x = lax.axis_index("kvh")
    y = ctx // 16
    z = lax.rem(ctx // 2, 8)
    c = lax.rem(ctx, 2)
    a = z + c * (y - z)
    b = y + c * (z - y)
    mine = c * HALF

    def at(aa, bb, cc):
        yy = bb + c * (aa - bb)
        zz = aa + c * (bb - aa)
        return ((yy * 8 + zz) * 2 + cc, x)

    sibling = (ctx + 1 - 2 * c, x)

    def ring_a(k):
        return lax.rem(a + k, HALF)

    def ring_b(k):
        return lax.rem(b + k, HALF)

    def dev_a(k):
        return at(ring_a(k), b, c)

    def dev_b(k):
        return at(a, ring_b(k), c)

    def dev_x(k):
        return (ctx, lax.rem(x + k, 4))

    pairs = (
        (hid_h, hid_v), (wq_h, wq_v), (gain_h, gain_v), (basis_h, basis_v), (lists_h, lists_v),
        (nk_h, nk_v), (nv_h, nv_v), (keys_h, keys_v), (vals_h, vals_v), (wo_h, wo_v),
    )
    fetch = [pltpu.make_async_copy(s, d, in_sem.at[i]) for i, (s, d) in enumerate(pairs)]
    for one in fetch:
        one.start()
    barrier = pltpu.get_barrier_semaphore()
    partners = [sibling] + [dev_a(k) for k in range(1, 8)] + [dev_b(k) for k in range(1, 8)]
    partners += [dev_x(k) for k in range(1, 4)]
    for who in partners:
        pl.semaphore_signal(barrier, inc=1, device_id=who, device_id_type=MESH)

    sends = []

    def send(src, dst, s_sem, r_sem, who):
        copy = pltpu.make_async_remote_copy(
            src_ref=src, dst_ref=dst, send_sem=s_sem, recv_sem=r_sem,
            device_id=who, device_id_type=MESH,
        )
        copy.start()
        sends.append(copy)
        return copy

    fetch[0].wait()
    fetch[1].wait()
    hid = jnp.concatenate(
        [hid_v[s].astype(F32) for s in range(STEPS)] + [jnp.zeros((SLOT - ROWS, hid_v.shape[2]), F32)],
        axis=0,
    ).astype(BF16)
    for h in range(HEADS):
        q_part[slot(h)] = jnp.dot(
            hid, wq_v[:, h * HD : (h + 1) * HD], preferred_element_type=F32
        )
    pl.semaphore_wait(barrier, len(partners))

    go = send(
        q_part.at[pl.ds(pl.multiple_of((HALF - mine) * SLOT, SLOT), HALF * SLOT)],
        q_core, core_s.at[0], core_r.at[0], sibling,
    )
    for one in fetch[2:7]:
        one.wait()

    list_rows[...] = jnp.full(list_rows.shape, -1, jnp.int32)
    for s in range(STEPS):
        for r in range(REQ):
            i = s * REQ + r
            list_rows[i : i + 1, :] = lists_v[s, r]
    nk_rows[...] = jnp.zeros(nk_rows.shape, F32)
    nv_rows[...] = jnp.zeros(nv_rows.shape, F32)
    for t in range(STEPS):
        for r in range(REQ):
            one_k = nk_v[t, r].astype(F32)
            one_v = nv_v[t, r].astype(F32)
            for s in range(t, STEPS):
                i = t * SLOT + s * REQ + r
                nk_rows[i : i + 1, :] = one_k
                nv_rows[i : i + 1, :] = one_v
    n_local = keys_v.shape[1] // BLK
    first = ctx * n_local
    lists = list_rows[...]
    for blk in range(n_local):
        hit = jnp.max(jnp.where(lists == first + blk, 1.0, 0.0), axis=1, keepdims=True)
        bias[:, blk * BLK : (blk + 1) * BLK] = jnp.broadcast_to(
            jnp.where(hit > 0.5, 0.0, NONE), (SLOT, BLK)
        )
    b_hi, b_mid, b_lo = split3(basis_v[0])
    for i, piece in enumerate((b_hi, b_mid, b_lo, b_hi, b_mid, b_hi)):
        rot[i * HD : (i + 1) * HD, :] = piece
    gain = gain_v[...].reshape(1, HD)

    go.wait_recv()
    q_half[...] = q_part[pl.ds(pl.multiple_of(mine * SLOT, SLOT), HALF * SLOT)] + q_core[...]
    got = [
        send(q_half.at[slot(ring_a(k))], q_rs.at[slot(k - 1)], rs_s.at[k - 1], rs_r.at[k - 1], dev_a(k))
        for k in range(1, 8)
    ]
    total = q_half[slot(a)]
    for k in range(1, 8):
        got[k - 1].wait_recv()
        total = total + q_rs[slot(k - 1)]
    q_own[slot(0)] = total
    got = [
        send(q_own.at[slot(0)], q_ex.at[slot(k - 1)], ex_s.at[k - 1], ex_r.at[k - 1], dev_b(k))
        for k in range(1, 8)
    ]
    for k in range(1, 8):
        got[k - 1].wait_recv()
        total = total + q_ex[slot(k - 1)]

    scale = HD ** (-0.5)
    norm = lax.rsqrt(jnp.mean(total * total, axis=1, keepdims=True) + 1e-06) * scale
    g_hi, g_mid, g_lo = split3(total * gain)
    turned = jnp.dot(
        jnp.concatenate([g_hi, g_hi, g_hi, g_mid, g_mid, g_lo], axis=1),
        rot[...],
        preferred_element_type=F32,
    )
    q_mine = turned * norm
    q_all[slot(mine + a)] = q_mine
    got = [
        send(
            q_all.at[slot(mine + a)], q_all.at[slot(mine + a)],
            ag_s.at[k - 1], ag_r.at[k - 1], dev_a(k),
        )
        for k in range(1, 8)
    ]
    for one in fetch[7:]:
        one.wait()
    for one in got:
        one.wait_recv()
    half = pl.ds(pl.multiple_of(mine * SLOT, SLOT), HALF * SLOT)
    go = send(q_all.at[half], q_all.at[half], core_s.at[1], core_r.at[1], sibling)
    go.wait_recv()

    lane48 = iota((STEPS * HEADS, HD), 1)
    lane16 = iota((HEADS, HD), 1)
    stat = jnp.zeros((HEADS, HD), F32)
    n_rows = STEPS * HEADS
    for r in range(REQ):
        q = jnp.concatenate(
            [q_all[pl.ds(s * REQ + r, HEADS, stride=SLOT), :] for s in range(STEPS)], axis=0
        )
        low = jnp.where(lane48 < RANK, q, 0.0)
        lhs = jnp.concatenate(split3(jnp.concatenate([q, low], axis=0)), axis=1)
        k_r = keys_v[r]
        scores = lax.dot_general(
            lhs, jnp.concatenate([k_r, k_r, k_r], axis=1), (((1,), (1,)), ((), ())),
            preferred_element_type=F32,
        )
        exact = jnp.concatenate(
            [
                scores[s * HEADS : (s + 1) * HEADS] + bias[s * REQ + r : s * REQ + r + 1, :]
                for s in range(STEPS)
            ],
            axis=0,
        )
        top = jnp.max(exact, axis=1, keepdims=True)
        probs = jnp.exp(exact - top)
        mass = jnp.sum(probs, axis=1, keepdims=True)
        acc = jnp.dot(probs.astype(BF16), vals_v[r], preferred_element_type=F32) / mass
        lse = top + jnp.log(mass)
        blocks = jnp.full((n_rows, HD), NONE, F32)
        for blk in range(n_local):
            part = scores[n_rows:, blk * BLK : (blk + 1) * BLK]
            peak = jnp.max(part, axis=1, keepdims=True)
            one = peak + jnp.log(jnp.sum(jnp.exp(part - peak), axis=1, keepdims=True))
            blocks = jnp.where(lane48 == blk, one, blocks)
        peak = jnp.max(blocks, axis=1, keepdims=True)
        low_lse = peak + jnp.log(jnp.sum(jnp.exp(blocks - peak), axis=1, keepdims=True))
        for s in range(STEPS):
            i = s * REQ + r
            rows = slice(s * HEADS, (s + 1) * HEADS)
            o_part[pl.ds(i, HEADS, stride=SLOT), :] = acc[rows]
            lse_all[slot(i)] = blocks[rows]
            stat = jnp.where(lane16 == i, lse[rows], stat)
            stat = jnp.where(lane16 == LOW + i, low_lse[rows], stat)
    o_part[pl.ds(STAT, HEADS, stride=SLOT), :] = stat
    for i in range(STAT + 1, SLOT):
        o_part[pl.ds(i, HEADS, stride=SLOT), :] = jnp.zeros((HEADS, HD), F32)

    go = send(
        o_part.at[pl.ds(pl.multiple_of((HALF - mine) * SLOT, SLOT), HALF * SLOT)],
        o_core, core_s.at[2], core_r.at[2], sibling,
    )
    row16 = iota((SLOT, 1), 0)
    fresh = [
        jnp.where(
            row16 >= t * REQ,
            jnp.sum(q_mine * nk_rows[slot(t)], axis=1, keepdims=True),
            NONE,
        )
        for t in range(STEPS)
    ]
    top = jnp.maximum(jnp.maximum(fresh[0], fresh[1]), fresh[2])
    new_w = [jnp.exp(f - top) for f in fresh]
    new_sum = new_w[0] + new_w[1] + new_w[2]
    new_o = sum(
        new_w[t].astype(BF16).astype(F32) * nv_rows[slot(t)] for t in range(STEPS)
    ) / new_sum
    diag = iota((SLOT, HD), 0) == iota((SLOT, HD), 1)
    new_row = jnp.sum(jnp.where(diag, top + jnp.log(new_sum), 0.0), axis=0, keepdims=True)
    new_row = jnp.where(iota((1, HD), 1) < ROWS, new_row, NONE)

    def is_stat():
        return iota((SLOT, HD), 0) == STAT

    go.wait_recv()
    mine_row = mine * SLOT
    stat0 = o_part[pl.ds(mine_row + STAT, HALF, stride=SLOT), :]
    stat1 = o_core[pl.ds(STAT, HALF, stride=SLOT), :]
    top = jnp.maximum(stat0, stat1)
    w0 = jnp.exp(stat0 - top)
    w1 = jnp.exp(stat1 - top)
    both = w0 + w1
    stat = top + jnp.log(both)
    w0 = w0 / both
    for h in range(HALF):
        f0 = column(w0[h : h + 1])
        o0 = o_part[slot(mine + h)]
        o1 = o_core[slot(h)]
        o_half[slot(h)] = jnp.where(is_stat(), stat[h : h + 1], o0 * f0 + o1 * (1.0 - f0))
    got = [
        send(o_half.at[slot(ring_a(k))], o_rs.at[slot(k - 1)], rs_s.at[6 + k], rs_r.at[6 + k], dev_a(k))
        for k in range(1, 8)
    ]

    def combine(parts):
        rows = [p[STAT : STAT + 1] if p.shape[0] == SLOT else p for p in parts]
        return rows

    def merge(outs, rows):
        top = rows[0]
        for one in rows[1:]:
            top = jnp.maximum(top, one)
        ws = [jnp.exp(one - top) for one in rows]
        total = sum(ws)
        inv = 1.0 / total
        res = sum(o * column(w * inv) for o, w in zip(outs, ws))
        return res, top + jnp.log(total)

    own = o_half[slot(a)]
    for one in got:
        one.wait_recv()
    outs = [own] + [o_rs[slot(k - 1)] for k in range(1, 8)]
    res, row = merge(outs, [p[STAT : STAT + 1] for p in outs])
    own = jnp.where(is_stat(), row, res)
    o_own[slot(0)] = own
    got = [
        send(o_own.at[slot(0)], o_ex.at[slot(k - 1)], ex_s.at[6 + k], ex_r.at[6 + k], dev_b(k))
        for k in range(1, 8)
    ]
    for one in got:
        one.wait_recv()
    outs = [own] + [o_ex[slot(k - 1)] for k in range(1, 8)]
    res, row = merge(outs + [new_o], [p[STAT : STAT + 1] for p in outs] + [new_row])
    o_all[slot(mine + a)] = jnp.where(is_stat(), row, res.astype(BF16).astype(F32))
    got = [
        send(
            o_all.at[slot(mine + a)], o_all.at[slot(mine + a)],
            ag_s.at[6 + k], ag_r.at[6 + k], dev_a(k),
        )
        for k in range(1, 8)
    ]
    for one in got:
        one.wait_recv()
    go = send(o_all.at[half], o_all.at[half], core_s.at[3], core_r.at[3], sibling)
    go.wait_recv()

    attn = jnp.concatenate([o_all[slot(h)].astype(BF16) for h in range(HEADS)], axis=1)
    term = jnp.dot(attn, wo_v[...], preferred_element_type=F32).astype(BF16).astype(F32)
    cols = term.shape[1]
    x_own[...] = jnp.zeros(x_own.shape, F32)
    x_own[:, :cols] = term
    got = [
        send(x_own, x_in.at[slot(k - 1)], x_s.at[k - 1], x_r.at[k - 1], dev_x(k))
        for k in range(1, 4)
    ]
    stat = o_all[pl.ds(STAT, HEADS, stride=SLOT), :]
    for s in range(STEPS):
        for r in range(REQ):
            i = s * REQ + r
            mass_o[s, r] = (lse_all[slot(i)] - stat[:, LOW + i : LOW + i + 1])[:, :n_local]
    for one in got:
        one.wait_recv()
    for k in range(1, 4):
        term = term + x_in[slot(k - 1), :cols]
    for s in range(STEPS):
        out_o[s] = term[s * REQ : (s + 1) * REQ].astype(BF16)
    for one in sends:
        one.wait_send()


def body(hidden, w_query, q_gain, basis, keys, values, new_keys, new_values, block_lists, w_out):
    n_tok = keys.shape[2]
    n_local = n_tok // BLK
    ops = (hidden, w_query, q_gain, basis, keys, values, new_keys, new_values, block_lists, w_out)
    slots = lambda n: pltpu.VMEM((n * SLOT, HD), F32)
    landing = [pltpu.VMEM(o.shape, o.dtype) for o in ops]
    landing[4] = landing[5] = pltpu.VMEM((REQ, n_tok, HD), BF16)
    dma = lambda n: pltpu.SemaphoreType.DMA((n,))

    def run(*refs):
        refs = list(refs)
        refs[4] = refs[4].at[:, 0]
        refs[5] = refs[5].at[:, 0]
        kernel(*refs)

    return pl.pallas_call(
        run,
        out_shape=(
            jax.ShapeDtypeStruct((STEPS, REQ, HEADS, n_local), F32),
            jax.ShapeDtypeStruct((STEPS, REQ, w_out.shape[1]), BF16),
        ),
        in_specs=[pl.BlockSpec(memory_space=pl.ANY)] * len(ops),
        out_specs=(pl.BlockSpec(memory_space=pltpu.VMEM),) * 2,
        scratch_shapes=landing
        + [
            pltpu.VMEM((SLOT, block_lists.shape[3]), jnp.int32),
            pltpu.VMEM((SLOT, n_tok), F32),
            slots(STEPS),
            slots(STEPS),
            pltpu.VMEM((6 * HD, HD), BF16),
        ]
        + [slots(n) for n in (16, 8, 8, 7, 1, 7, 16)]
        + [slots(n) for n in (16, 8, 8, 7, 1, 7, 16, 12)]
        + [slots(1), slots(3)]
        + [dma(n) for n in (10, 4, 4, 14, 14, 14, 14, 14, 14, 3, 3)],
        compiler_params=pltpu.CompilerParams(
            collective_id=0, has_side_effects=True, vmem_limit_bytes=48 * 2**20
        ),
        name="decode",
    )(*ops)


def solution(mesh):
    placed = (
        P(None, None, "ctx"),
        P("ctx", "kvh"),
        P(),
        P("kvh", None, None),
        P(None, "kvh", "ctx", None),
        P(None, "kvh", "ctx", None),
        P(None, None, "kvh", None),
        P(None, None, "kvh", None),
        P(None, None, "kvh", None),
        P("kvh", "ctx"),
    )
    return jax.shard_map(
        body,
        mesh=mesh,
        in_specs=placed,
        out_specs=(P(None, None, "kvh", "ctx"), P(None, None, "ctx")),
        check_vma=False,
    )
```

```python
import jax
import jax.numpy as jnp
from jax import lax
from jax.experimental import pallas as pl
from jax.experimental.pallas import tpu as pltpu
from jax.sharding import PartitionSpec as P

RANK = 32
BLK = 128
STEPS = 3
REQ = 4
ROWS = STEPS * REQ
SLOT = 16
STAT = 12
LOW = 16
HEADS = 16
HALF = 8
HD = 128
NONE = -1e30
FAR_FIRST = (4, 3, 5, 2, 6, 1, 7)
MESH = pl.DeviceIdType.MESH
F32 = jnp.float32
BF16 = jnp.bfloat16


def split3(x):
    hi = x.astype(BF16)
    rest = x - hi.astype(F32)
    mid = rest.astype(BF16)
    lo = (rest - mid.astype(F32)).astype(BF16)
    return hi, mid, lo


def slot(i):
    if isinstance(i, int):
        return pl.ds(i * SLOT, SLOT)
    return pl.ds(pl.multiple_of(i * SLOT, SLOT), SLOT)


def rows_of(i):
    if isinstance(i, int):
        return pl.ds(i * SLOT, ROWS)
    return pl.ds(pl.multiple_of(i * SLOT, SLOT), ROWS)


def iota(shape, dim):
    return lax.broadcasted_iota(jnp.int32, shape, dim)


def column(row):
    diag = iota((SLOT, HD), 0) == iota((SLOT, HD), 1)
    return jnp.sum(jnp.where(diag, row, 0.0), axis=1, keepdims=True)


def stat_of(x):
    return x[STAT : STAT + 1] + x[STAT + 1 : STAT + 2] + x[STAT + 2 : STAT + 3]


def with_stat(x, row):
    i = iota((SLOT, HD), 0)
    hi, mid, lo = (p.astype(F32) for p in split3(row))
    tail = jnp.where(i == STAT, hi, jnp.where(i == STAT + 1, mid, lo))
    return jnp.where(i < ROWS, x, jnp.where(i < STAT + 3, tail, 0.0)).astype(BF16)


def merge(outs, rows):
    top = rows[0]
    for one in rows[1:]:
        top = jnp.maximum(top, one)
    ws = [jnp.exp(one - top) for one in rows]
    total = sum(ws)
    inv = 1.0 / total
    res = sum(o * column(w * inv) for o, w in zip(outs, ws))
    return res, top + jnp.log(total)


def kernel(
    hid_h, wq_h, gain_h, basis_h, keys_h, vals_h, nk_h, nv_h, lists_h, wo_h,
    mass_o, out_o,
    hid_v, wq_v, gain_v, basis_v, keys_v, vals_v, nk_v, nv_v, lists_v, wo_v,
    list_rows, bias, nk_rows, nv_rows, rot, wo_t,
    q_part, q_rs, q_own, q_ex, q_all,
    o_wide, lse_all,
    o_part, o_rs, o_own, o_ex, o_all, x_own, x_in,
    in_sem, rs_s, rs_r, ex_s, ex_r, ag_s, ag_r, x_s, x_r,
):
    ctx = lax.axis_index("ctx")
    x = lax.axis_index("kvh")
    y = ctx // 16
    z = lax.rem(ctx // 2, 8)
    c = lax.rem(ctx, 2)
    a = z + c * (y - z)
    b = y + c * (z - y)
    mine = c * HALF + a
    theirs = (1 - c) * HALF

    def at(aa, bb, cc):
        yy = bb + c * (aa - bb)
        zz = aa + c * (bb - aa)
        return ((yy * 8 + zz) * 2 + cc, x)

    def ring_a(k):
        return lax.rem(a + k, HALF)

    def ring_b(k):
        return lax.rem(b + k, HALF)

    def dev_a(k):
        return at(ring_a(k), b, c)

    def dev_b(k):
        return at(a, ring_b(k), c)

    def cross_a(k):
        return at(ring_a(k), b, 1 - c)

    def cross_b(k):
        return at(a, ring_b(k), 1 - c)

    def dev_x(k):
        return (ctx, lax.rem(x + k, 4))

    pairs = (
        (hid_h, hid_v), (wq_h, wq_v), (gain_h, gain_v), (basis_h, basis_v), (lists_h, lists_v),
        (nk_h, nk_v), (nv_h, nv_v), (wo_h, wo_v), (keys_h, keys_v), (vals_h, vals_v),
    )
    fetch = [pltpu.make_async_copy(s, d, in_sem.at[i]) for i, (s, d) in enumerate(pairs)]
    for one in fetch:
        one.start()
    barrier = pltpu.get_barrier_semaphore()
    partners = []
    for k in FAR_FIRST:
        partners += [dev_a(k), dev_b(k), cross_a(k), cross_b(k)]
    partners += [dev_x(2), dev_x(1), dev_x(3), cross_a(0)]
    for who in partners:
        pl.semaphore_signal(barrier, inc=1, device_id=who, device_id_type=MESH)

    sends = []

    def send(src, dst, s_sem, r_sem, who):
        copy = pltpu.make_async_remote_copy(
            src_ref=src, dst_ref=dst, send_sem=s_sem, recv_sem=r_sem,
            device_id=who, device_id_type=MESH,
        )
        copy.start()
        sends.append(copy)
        return copy

    def scatter(part, into, cut, base):
        got = {}
        for k in FAR_FIRST + (0,):
            if k:
                got[k - 1] = send(
                    part.at[cut(c * HALF + ring_a(k))], into.at[cut(k - 1)],
                    rs_s.at[base + k - 1], rs_r.at[base + k - 1], dev_a(k),
                )
            got[7 + k] = send(
                part.at[cut(theirs + ring_b(k))], into.at[cut(7 + k)],
                rs_s.at[base + 7 + k], rs_r.at[base + 7 + k], cross_b(k),
            )
        return [got[i] for i in range(15)]

    def gather(buf, cut, base):
        got = {}
        for k in FAR_FIRST + (0,):
            if k:
                got[k - 1] = send(
                    buf.at[cut(mine)], buf.at[cut(mine)],
                    ag_s.at[base + k - 1], ag_r.at[base + k - 1], dev_a(k),
                )
            got[7 + k] = send(
                buf.at[cut(mine)], buf.at[cut(mine)],
                ag_s.at[base + 7 + k], ag_r.at[base + 7 + k], cross_a(k),
            )
        return [got[i] for i in range(15)]

    def exchange(own, into, cut, base):
        got = {}
        for k in FAR_FIRST:
            got[k - 1] = send(
                own.at[cut(0)], into.at[cut(k - 1)],
                ex_s.at[base + k - 1], ex_r.at[base + k - 1], dev_b(k),
            )
        return [got[i] for i in range(7)]

    fetch[0].wait()
    fetch[1].wait()
    hid = jnp.concatenate(
        [hid_v[s].astype(F32) for s in range(STEPS)] + [jnp.zeros((SLOT - ROWS, hid_v.shape[2]), F32)],
        axis=0,
    ).astype(BF16)
    for h in range(HEADS):
        q_part[slot(h)] = jnp.dot(
            hid, wq_v[:, h * HD : (h + 1) * HD], preferred_element_type=F32
        )
    pl.semaphore_wait(barrier, len(partners))

    got = scatter(q_part, q_rs, rows_of, 0)
    for one in fetch[2:8]:
        one.wait()

    list_rows[...] = jnp.full(list_rows.shape, -1, jnp.int32)
    for s in range(STEPS):
        for r in range(REQ):
            i = s * REQ + r
            list_rows[i : i + 1, :] = lists_v[s, r]
    nk_rows[...] = jnp.zeros(nk_rows.shape, F32)
    nv_rows[...] = jnp.zeros(nv_rows.shape, F32)
    for t in range(STEPS):
        one_k = nk_v[t].astype(F32)
        one_v = nv_v[t].astype(F32)
        for s in range(t, STEPS):
            i = t * SLOT + s * REQ
            nk_rows[i : i + REQ, :] = one_k
            nv_rows[i : i + REQ, :] = one_v
    n_local = keys_v.shape[1] // BLK
    first = ctx * n_local
    lists = list_rows[...]
    for blk in range(n_local):
        hit = jnp.max(jnp.where(lists == first + blk, 1.0, 0.0), axis=1, keepdims=True)
        bias[:, blk * BLK : (blk + 1) * BLK] = jnp.broadcast_to(
            jnp.where(hit > 0.5, 0.0, NONE), (SLOT, BLK)
        )
    b_hi, b_mid, b_lo = split3(basis_v[0])
    for i, piece in enumerate((b_hi, b_mid, b_lo, b_hi, b_mid, b_hi)):
        rot[i * HD : (i + 1) * HD, :] = piece
    gain = gain_v[...].reshape(1, HD)
    wo_t[...] = wo_v[...].astype(F32).T.astype(BF16)

    total = q_part[slot(mine)]
    for k in range(15):
        got[k].wait_recv()
        total = total + q_rs[slot(k)]
    total = jnp.where(iota((SLOT, HD), 0) < ROWS, total, 0.0)
    q_own[...] = total
    got = exchange(q_own, q_ex, rows_of, 0)
    for k in range(7):
        got[k].wait_recv()
        total = total + q_ex[slot(k)]
    total = jnp.where(iota((SLOT, HD), 0) < ROWS, total, 0.0)

    scale = HD ** (-0.5)
    norm = lax.rsqrt(jnp.mean(total * total, axis=1, keepdims=True) + 1e-06) * scale
    g_hi, g_mid, g_lo = split3(total * gain)
    turned = jnp.dot(
        jnp.concatenate([g_hi, g_hi, g_hi, g_mid, g_mid, g_lo], axis=1),
        rot[...],
        preferred_element_type=F32,
    )
    q_mine = turned * norm
    q_all[slot(mine)] = q_mine
    got = gather(q_all, rows_of, 0)
    for one in fetch[8:]:
        one.wait()
    for one in got:
        one.wait_recv()

    lane48 = iota((STEPS * HEADS, HD), 1)
    lane16 = iota((HEADS, HD), 1)
    stat = jnp.zeros((HEADS, HD), F32)
    n_rows = STEPS * HEADS
    for r in range(REQ):
        q = jnp.concatenate(
            [q_all[pl.ds(s * REQ + r, HEADS, stride=SLOT), :] for s in range(STEPS)], axis=0
        )
        low = jnp.where(lane48 < RANK, q, 0.0)
        lhs = jnp.concatenate(split3(jnp.concatenate([q, low], axis=0)), axis=1)
        k_r = keys_v[r]
        scores = lax.dot_general(
            lhs, jnp.concatenate([k_r, k_r, k_r], axis=1), (((1,), (1,)), ((), ())),
            preferred_element_type=F32,
        )
        exact = jnp.concatenate(
            [
                scores[s * HEADS : (s + 1) * HEADS] + bias[s * REQ + r : s * REQ + r + 1, :]
                for s in range(STEPS)
            ],
            axis=0,
        )
        top = jnp.max(exact, axis=1, keepdims=True)
        probs = jnp.exp(exact - top)
        mass = jnp.sum(probs, axis=1, keepdims=True)
        acc = jnp.dot(probs.astype(BF16), vals_v[r], preferred_element_type=F32) / mass
        lse = top + jnp.log(mass)
        blocks = jnp.full((n_rows, HD), NONE, F32)
        for blk in range(n_local):
            part = scores[n_rows:, blk * BLK : (blk + 1) * BLK]
            peak = jnp.max(part, axis=1, keepdims=True)
            one = peak + jnp.log(jnp.sum(jnp.exp(part - peak), axis=1, keepdims=True))
            blocks = jnp.where(lane48 == blk, one, blocks)
        peak = jnp.max(blocks, axis=1, keepdims=True)
        low_lse = peak + jnp.log(jnp.sum(jnp.exp(blocks - peak), axis=1, keepdims=True))
        for s in range(STEPS):
            i = s * REQ + r
            rows = slice(s * HEADS, (s + 1) * HEADS)
            o_wide[pl.ds(i, HEADS, stride=SLOT), :] = acc[rows]
            lse_all[slot(i)] = blocks[rows]
            stat = jnp.where(lane16 == i, lse[rows], stat)
            stat = jnp.where(lane16 == LOW + i, low_lse[rows], stat)
    for i, piece in enumerate(split3(stat)):
        o_wide[pl.ds(STAT + i, HEADS, stride=SLOT), :] = piece.astype(F32)
    o_wide[pl.ds(SLOT - 1, HEADS, stride=SLOT), :] = jnp.zeros((HEADS, HD), F32)
    o_part[...] = o_wide[...].astype(BF16)

    got = scatter(o_part, o_rs, slot, 15)
    row16 = iota((SLOT, 1), 0)
    fresh = [
        jnp.where(
            row16 >= t * REQ,
            jnp.sum(q_mine * nk_rows[slot(t)], axis=1, keepdims=True),
            NONE,
        )
        for t in range(STEPS)
    ]
    top = jnp.maximum(jnp.maximum(fresh[0], fresh[1]), fresh[2])
    new_w = [jnp.exp(f - top) for f in fresh]
    new_sum = new_w[0] + new_w[1] + new_w[2]
    new_o = sum(
        new_w[t].astype(BF16).astype(F32) * nv_rows[slot(t)] for t in range(STEPS)
    ) / new_sum
    diag = iota((SLOT, HD), 0) == iota((SLOT, HD), 1)
    new_row = jnp.sum(jnp.where(diag, top + jnp.log(new_sum), 0.0), axis=0, keepdims=True)
    new_row = jnp.where(iota((1, HD), 1) < ROWS, new_row, NONE)

    for one in got:
        one.wait_recv()
    outs = [o_wide[slot(mine)]] + [o_rs[slot(k)].astype(F32) for k in range(15)]
    res, row = merge(outs, [stat_of(p) for p in outs])
    o_own[...] = with_stat(res, row)
    got = exchange(o_own, o_ex, slot, 7)
    for one in got:
        one.wait_recv()
    outs = [o_ex[slot(k)].astype(F32) for k in range(7)]
    res, row = merge([res, new_o] + outs, [row, new_row] + [stat_of(p) for p in outs])
    o_all[slot(mine)] = with_stat(res, row)
    got = gather(o_all, slot, 15)
    for one in got:
        one.wait_recv()

    attn = jnp.concatenate([o_all[slot(h)] for h in range(HEADS)], axis=1)
    term = jnp.dot(attn, wo_t[...], preferred_element_type=F32).astype(BF16)
    cols = term.shape[1]
    x_own[:, :cols] = term
    got = [
        send(x_own, x_in.at[slot(k - 1)], x_s.at[k - 1], x_r.at[k - 1], dev_x(k))
        for k in (2, 1, 3)
    ]
    o_wide[...] = o_all[...].astype(F32)
    stat = sum(o_wide[pl.ds(STAT + i, HEADS, stride=SLOT), :] for i in range(3))
    for s in range(STEPS):
        for r in range(REQ):
            i = s * REQ + r
            mass_o[s, r] = (lse_all[slot(i)] - stat[:, LOW + i : LOW + i + 1])[:, :n_local]
    for one in got:
        one.wait_recv()
    term = term.astype(F32)
    for k in range(1, 4):
        term = term + x_in[slot(k - 1), :cols].astype(F32)
    for s in range(STEPS):
        out_o[s] = term[s * REQ : (s + 1) * REQ].astype(BF16)
    for one in sends:
        one.wait_send()


def body(hidden, w_query, q_gain, basis, keys, values, new_keys, new_values, block_lists, w_out):
    n_tok = keys.shape[2]
    n_local = n_tok // BLK
    new_keys, new_values = new_keys[:, :, 0], new_values[:, :, 0]
    ops = (hidden, w_query, q_gain, basis, keys, values, new_keys, new_values, block_lists, w_out.T)
    slots = lambda n, kind=F32: pltpu.VMEM((n * SLOT, HD), kind)
    landing = [pltpu.VMEM(o.shape, o.dtype) for o in ops]
    landing[4] = landing[5] = pltpu.VMEM((REQ, n_tok, HD), BF16)
    dma = lambda n: pltpu.SemaphoreType.DMA((n,))

    def run(*refs):
        refs = list(refs)
        refs[4] = refs[4].at[:, 0]
        refs[5] = refs[5].at[:, 0]
        kernel(*refs)

    return pl.pallas_call(
        run,
        out_shape=(
            jax.ShapeDtypeStruct((STEPS, REQ, HEADS, n_local), F32),
            jax.ShapeDtypeStruct((STEPS, REQ, w_out.shape[1]), BF16),
        ),
        in_specs=[pl.BlockSpec(memory_space=pltpu.HBM)] * len(ops),
        out_specs=(pl.BlockSpec(memory_space=pltpu.VMEM),) * 2,
        scratch_shapes=landing
        + [
            pltpu.VMEM((SLOT, block_lists.shape[3]), jnp.int32),
            pltpu.VMEM((SLOT, n_tok), F32),
            slots(STEPS),
            slots(STEPS),
            pltpu.VMEM((6 * HD, HD), BF16),
            pltpu.VMEM((w_out.shape[0], w_out.shape[1]), BF16),
        ]
        + [slots(n) for n in (16, 15, 1, 7, 16, 16, 12)]
        + [slots(n, BF16) for n in (16, 15, 1, 7, 16, 1, 3)]
        + [dma(n) for n in (10, 30, 30, 14, 14, 30, 30, 3, 3)],
        compiler_params=pltpu.CompilerParams(
            collective_id=0, has_side_effects=True, vmem_limit_bytes=60 * 2**20
        ),
        name="decode",
    )(*ops)


def solution(mesh):
    placed = (
        P(None, None, "ctx"),
        P("ctx", "kvh"),
        P(),
        P("kvh", None, None),
        P(None, "kvh", "ctx", None),
        P(None, "kvh", "ctx", None),
        P(None, None, "kvh", None),
        P(None, None, "kvh", None),
        P(None, None, "kvh", None),
        P("kvh", "ctx"),
    )
    return jax.shard_map(
        body,
        mesh=mesh,
        in_specs=placed,
        out_specs=(P(None, None, "kvh", "ctx"), P(None, None, "ctx")),
        check_vma=False,
    )
```

```python
import jax
import jax.numpy as jnp
from jax import lax
from jax.experimental import pallas as pl
from jax.experimental.pallas import tpu as pltpu
from jax.sharding import PartitionSpec as P

RANK = 32
BLK = 128
STEPS = 3
REQ = 4
ROWS = STEPS * REQ
SLOT = 16
STAT = 12
LOW = 16
HEADS = 16
HALF = 8
HD = 128
NONE = -1e30
FAR_FIRST = (4, 3, 5, 2, 6, 1, 7)
MESH = pl.DeviceIdType.MESH
F32 = jnp.float32
BF16 = jnp.bfloat16


def split3(x):
    hi = x.astype(BF16)
    rest = x - hi.astype(F32)
    mid = rest.astype(BF16)
    lo = (rest - mid.astype(F32)).astype(BF16)
    return hi, mid, lo


def slot(i):
    if isinstance(i, int):
        return pl.ds(i * SLOT, SLOT)
    return pl.ds(pl.multiple_of(i * SLOT, SLOT), SLOT)


def rows_of(i):
    if isinstance(i, int):
        return pl.ds(i * SLOT, ROWS)
    return pl.ds(pl.multiple_of(i * SLOT, SLOT), ROWS)


def iota(shape, dim):
    return lax.broadcasted_iota(jnp.int32, shape, dim)


def column(row):
    diag = iota((SLOT, HD), 0) == iota((SLOT, HD), 1)
    return jnp.sum(jnp.where(diag, row, 0.0), axis=1, keepdims=True)


def stat_of(x):
    return x[STAT : STAT + 1] + x[STAT + 1 : STAT + 2] + x[STAT + 2 : STAT + 3]


def with_stat(x, row):
    i = iota((SLOT, HD), 0)
    hi, mid, lo = (p.astype(F32) for p in split3(row))
    tail = jnp.where(i == STAT, hi, jnp.where(i == STAT + 1, mid, lo))
    return jnp.where(i < ROWS, x, jnp.where(i < STAT + 3, tail, 0.0)).astype(BF16)


def merge(outs, rows):
    top = rows[0]
    for one in rows[1:]:
        top = jnp.maximum(top, one)
    ws = [jnp.exp(one - top) for one in rows]
    total = sum(ws)
    inv = 1.0 / total
    res = sum(o * column(w * inv) for o, w in zip(outs, ws))
    return res, top + jnp.log(total)


def kernel(
    hid_h, wq_h, gain_h, basis_h, keys_h, vals_h, nk_h, nv_h, lists_h, wo_h,
    mass_o, out_o,
    hid_v, wq_v, gain_v, basis_v, keys_v, vals_v, nk_v, nv_v, lists_v, wo_v,
    list_rows, bias, nk_rows, nv_rows, rot, wo_t, keys_t, low_keys, mass_v, out_v,
    q_part, q_rs, q_own, q_ex, q_all,
    o_wide, lse_all,
    o_part, o_rs, o_own, o_ex, o_all, x_own, x_in,
    in_sem, out_sem, rs_s, rs_r, ex_s, ex_r, ag_s, ag_r, x_s, x_r,
):
    ctx = lax.axis_index("ctx")
    x = lax.axis_index("kvh")
    y = ctx // 16
    z = lax.rem(ctx // 2, 8)
    c = lax.rem(ctx, 2)
    a = z + c * (y - z)
    b = y + c * (z - y)
    mine = c * HALF + a
    theirs = (1 - c) * HALF

    def at(aa, bb, cc):
        yy = bb + c * (aa - bb)
        zz = aa + c * (bb - aa)
        return ((yy * 8 + zz) * 2 + cc, x)

    def ring_a(k):
        return lax.rem(a + k, HALF)

    def ring_b(k):
        return lax.rem(b + k, HALF)

    def dev_a(k):
        return at(ring_a(k), b, c)

    def dev_b(k):
        return at(a, ring_b(k), c)

    def cross_a(k):
        return at(ring_a(k), b, 1 - c)

    def cross_b(k):
        return at(a, ring_b(k), 1 - c)

    def dev_x(k):
        return (ctx, lax.rem(x + k, 4))

    barrier = pltpu.get_barrier_semaphore()
    partners = []
    for k in FAR_FIRST:
        partners += [dev_a(k), dev_b(k), cross_a(k), cross_b(k)]
    partners += [dev_x(2), dev_x(1), dev_x(3), cross_a(0)]
    for who in partners:
        pl.semaphore_signal(barrier, inc=1, device_id=who, device_id_type=MESH)
    pairs = (
        (hid_h, hid_v), (wq_h, wq_v), (gain_h, gain_v), (basis_h, basis_v), (lists_h, lists_v),
        (nk_h, nk_v), (nv_h, nv_v), (wo_h, wo_v), (keys_h, keys_v), (vals_h, vals_v),
    )
    fetch = [pltpu.make_async_copy(s, d, in_sem.at[i]) for i, (s, d) in enumerate(pairs)]
    for one in fetch:
        one.start()

    sends = []

    def send(src, dst, s_sem, r_sem, who):
        copy = pltpu.make_async_remote_copy(
            src_ref=src, dst_ref=dst, send_sem=s_sem, recv_sem=r_sem,
            device_id=who, device_id_type=MESH,
        )
        copy.start()
        sends.append(copy)
        return copy

    def scatter(part, into, cut, base):
        got = {}
        for k in FAR_FIRST + (0,):
            if k:
                got[k - 1] = send(
                    part.at[cut(c * HALF + ring_a(k))], into.at[cut(k - 1)],
                    rs_s.at[base + k - 1], rs_r.at[base + k - 1], dev_a(k),
                )
            got[7 + k] = send(
                part.at[cut(theirs + ring_b(k))], into.at[cut(7 + k)],
                rs_s.at[base + 7 + k], rs_r.at[base + 7 + k], cross_b(k),
            )
        return [got[i] for i in range(15)]

    def gather(buf, cut, base):
        got = {}
        for k in FAR_FIRST + (0,):
            if k:
                got[k - 1] = send(
                    buf.at[cut(mine)], buf.at[cut(mine)],
                    ag_s.at[base + k - 1], ag_r.at[base + k - 1], dev_a(k),
                )
            got[7 + k] = send(
                buf.at[cut(mine)], buf.at[cut(mine)],
                ag_s.at[base + 7 + k], ag_r.at[base + 7 + k], cross_a(k),
            )
        return [got[i] for i in range(15)]

    def exchange(own, into, cut, base):
        got = {}
        for k in FAR_FIRST:
            got[k - 1] = send(
                own.at[cut(0)], into.at[cut(k - 1)],
                ex_s.at[base + k - 1], ex_r.at[base + k - 1], dev_b(k),
            )
        return [got[i] for i in range(7)]

    fetch[0].wait()
    fetch[1].wait()
    hid = jnp.concatenate(
        [hid_v[s].astype(F32) for s in range(STEPS)] + [jnp.zeros((SLOT - ROWS, hid_v.shape[2]), F32)],
        axis=0,
    ).astype(BF16)
    for h in range(HEADS):
        q_part[slot(h)] = jnp.dot(
            hid, wq_v[:, h * HD : (h + 1) * HD], preferred_element_type=F32
        )
    pl.semaphore_wait(barrier, len(partners))

    got = scatter(q_part, q_rs, rows_of, 0)
    for one in fetch[2:9]:
        one.wait()

    list_rows[...] = jnp.full(list_rows.shape, -1, jnp.int32)
    for s in range(STEPS):
        for r in range(REQ):
            i = s * REQ + r
            list_rows[i : i + 1, :] = lists_v[s, r]
    nk_rows[...] = jnp.zeros(nk_rows.shape, F32)
    nv_rows[...] = jnp.zeros(nv_rows.shape, F32)
    for t in range(STEPS):
        one_k = nk_v[t].astype(F32)
        one_v = nv_v[t].astype(F32)
        for s in range(t, STEPS):
            i = t * SLOT + s * REQ
            nk_rows[i : i + REQ, :] = one_k
            nv_rows[i : i + REQ, :] = one_v
    n_local = keys_v.shape[1] // BLK
    first = ctx * n_local
    lists = list_rows[...]
    for blk in range(n_local):
        hit = jnp.max(jnp.where(lists == first + blk, 1.0, 0.0), axis=1, keepdims=True)
        bias[:, blk * BLK : (blk + 1) * BLK] = jnp.broadcast_to(
            jnp.where(hit > 0.5, 0.0, NONE), (SLOT, BLK)
        )
    b_hi, b_mid, b_lo = split3(basis_v[0])
    for i, piece in enumerate((b_hi, b_mid, b_lo, b_hi, b_mid, b_hi)):
        rot[i * HD : (i + 1) * HD, :] = piece
    gain = gain_v[...].reshape(1, HD)
    wo_t[...] = wo_v[...].astype(F32).T.astype(BF16)
    for r in range(REQ):
        keys_t[r] = keys_v[r].T

    total = q_part[slot(mine)]
    for k in range(15):
        got[k].wait_recv()
        total = total + q_rs[slot(k)]
    total = jnp.where(iota((SLOT, HD), 0) < ROWS, total, 0.0)
    q_own[...] = total
    got = exchange(q_own, q_ex, rows_of, 0)
    copies = (iota((HD, HD), 0) == lax.rem(iota((HD, HD), 1), RANK)).astype(F32).astype(BF16)
    for r in range(REQ):
        low_keys[r // 2, :, (r % 2) * HD : (r % 2 + 1) * HD] = jnp.dot(
            keys_v[r], copies, preferred_element_type=F32
        ).astype(BF16)
    for k in range(7):
        got[k].wait_recv()
        total = total + q_ex[slot(k)]
    total = jnp.where(iota((SLOT, HD), 0) < ROWS, total, 0.0)

    scale = HD ** (-0.5)
    norm = lax.rsqrt(jnp.mean(total * total, axis=1, keepdims=True) + 1e-06) * scale
    g_hi, g_mid, g_lo = split3(total * gain)
    turned = jnp.dot(
        jnp.concatenate([g_hi, g_hi, g_hi, g_mid, g_mid, g_lo], axis=1),
        rot[...],
        preferred_element_type=F32,
    )
    q_mine = turned * norm
    q_all[slot(mine)] = q_mine
    got = gather(q_all, rows_of, 0)
    fetch[9].wait()
    for one in got:
        one.wait_recv()

    lane16 = iota((HEADS, HD), 1)
    stat = jnp.zeros((HEADS, HD), F32)
    n_rows = STEPS * HEADS
    q_of = [
        jnp.concatenate(
            [q_all[pl.ds(s * REQ + r, HEADS, stride=SLOT), :] for s in range(STEPS)], axis=0
        )
        for r in range(REQ)
    ]
    parts_of = [split3(q) for q in q_of]
    for r in range(REQ):
        scores = jnp.dot(
            jnp.concatenate(parts_of[r], axis=0), keys_t[r], preferred_element_type=F32
        )
        scores = scores[:n_rows] + scores[n_rows : 2 * n_rows] + scores[2 * n_rows :]
        exact = jnp.concatenate(
            [
                scores[s * HEADS : (s + 1) * HEADS] + bias[s * REQ + r : s * REQ + r + 1, :]
                for s in range(STEPS)
            ],
            axis=0,
        )
        top = jnp.max(exact, axis=1, keepdims=True)
        probs = jnp.exp(exact - top)
        mass = jnp.sum(probs, axis=1, keepdims=True)
        acc = jnp.dot(probs.astype(BF16), vals_v[r], preferred_element_type=F32) / mass
        lse = top + jnp.log(mass)
        for s in range(STEPS):
            i = s * REQ + r
            rows = slice(s * HEADS, (s + 1) * HEADS)
            o_wide[pl.ds(i, HEADS, stride=SLOT), :] = acc[rows]
            stat = jnp.where(lane16 == i, lse[rows], stat)
    lane48 = iota((n_rows, HD), 1)
    for pair in range(REQ // 2):
        sides = []
        for half in range(2):
            hi, mid, lo = (p.astype(F32) for p in parts_of[2 * pair + half])
            packed = jnp.where(
                lane48 < RANK,
                hi,
                jnp.where(
                    lane48 < 2 * RANK,
                    pltpu.roll(mid, RANK, 1),
                    jnp.where(lane48 < 3 * RANK, pltpu.roll(lo, 2 * RANK, 1), 0.0),
                ),
            )
            blank = jnp.zeros((HD // 2, HD), F32)
            packed = jnp.concatenate([packed, blank[: HD // 2 - n_rows]], axis=0)
            sides.append(jnp.concatenate([blank, packed] if half else [packed, blank], axis=0).T)
        columns = jnp.concatenate(sides, axis=0).astype(BF16)
        rows = []
        for blk in range(n_local):
            part = jnp.dot(
                low_keys[pair, blk * BLK : (blk + 1) * BLK], columns, preferred_element_type=F32
            )
            peak = jnp.max(part, axis=0, keepdims=True)
            rows.append(peak + jnp.log(jnp.sum(jnp.exp(part - peak), axis=0, keepdims=True)))
        blocks = jnp.concatenate(rows, axis=0)
        peak = jnp.max(blocks, axis=0, keepdims=True)
        low_lse = peak + jnp.log(jnp.sum(jnp.exp(blocks - peak), axis=0, keepdims=True))
        lse_all[pair, :n_local] = blocks
        low_lse = jnp.broadcast_to(low_lse, (8, HD)).T
        for half in range(2):
            for s in range(STEPS):
                at_row = half * (HD // 2) + s * HEADS
                stat = jnp.where(
                    lane16 == LOW + s * REQ + 2 * pair + half,
                    low_lse[at_row : at_row + HEADS, :1],
                    stat,
                )
    for i, piece in enumerate(split3(stat)):
        o_wide[pl.ds(STAT + i, HEADS, stride=SLOT), :] = piece.astype(F32)
    o_wide[pl.ds(SLOT - 1, HEADS, stride=SLOT), :] = jnp.zeros((HEADS, HD), F32)
    o_part[...] = o_wide[...].astype(BF16)

    got = scatter(o_part, o_rs, slot, 15)
    row16 = iota((SLOT, 1), 0)
    fresh = [
        jnp.where(
            row16 >= t * REQ,
            jnp.sum(q_mine * nk_rows[slot(t)], axis=1, keepdims=True),
            NONE,
        )
        for t in range(STEPS)
    ]
    top = jnp.maximum(jnp.maximum(fresh[0], fresh[1]), fresh[2])
    new_w = [jnp.exp(f - top) for f in fresh]
    new_sum = new_w[0] + new_w[1] + new_w[2]
    new_o = sum(
        new_w[t].astype(BF16).astype(F32) * nv_rows[slot(t)] for t in range(STEPS)
    ) / new_sum
    diag = iota((SLOT, HD), 0) == iota((SLOT, HD), 1)
    new_row = jnp.sum(jnp.where(diag, top + jnp.log(new_sum), 0.0), axis=0, keepdims=True)
    new_row = jnp.where(iota((1, HD), 1) < ROWS, new_row, NONE)

    for one in got:
        one.wait_recv()
    outs = [o_wide[slot(mine)]] + [o_rs[slot(k)].astype(F32) for k in range(15)]
    res, row = merge(outs, [stat_of(p) for p in outs])
    o_own[...] = with_stat(res, row)
    got = exchange(o_own, o_ex, slot, 7)
    for one in got:
        one.wait_recv()
    outs = [o_ex[slot(k)].astype(F32) for k in range(7)]
    res, row = merge([res, new_o] + outs, [row, new_row] + [stat_of(p) for p in outs])
    o_all[slot(mine)] = with_stat(res, row)
    got = gather(o_all, slot, 15)
    for one in got:
        one.wait_recv()

    attn = jnp.concatenate([o_all[slot(h)] for h in range(HEADS)], axis=1)
    term = jnp.dot(attn, wo_t[...], preferred_element_type=F32).astype(BF16)
    cols = term.shape[1]
    x_own[:, :cols] = term
    got = [
        send(x_own, x_in.at[slot(k - 1)], x_s.at[k - 1], x_r.at[k - 1], dev_x(k))
        for k in (2, 1, 3)
    ]
    o_wide[...] = o_all[...].astype(F32)
    stat = sum(o_wide[pl.ds(STAT + i, HEADS, stride=SLOT), :] for i in range(3))
    stat = jnp.concatenate([stat, jnp.zeros((HD - HEADS, HD), F32)], axis=0).T
    for r in range(REQ):
        blocks = lse_all[r // 2]
        for s in range(STEPS):
            i = LOW + s * REQ + r
            at_lane = (r % 2) * (HD // 2) + s * HEADS
            moved = pltpu.roll(blocks, HD - at_lane, 1) if at_lane else blocks
            mass_v[s, :, r, :] = (moved - stat[i : i + 1])[:n_local, :HEADS]
    mass_out = pltpu.make_async_copy(mass_v, mass_o, out_sem.at[0])
    mass_out.start()
    for one in got:
        one.wait_recv()
    term = term.astype(F32)
    for k in range(1, 4):
        term = term + x_in[slot(k - 1), :cols].astype(F32)
    for s in range(STEPS):
        out_v[s] = term[s * REQ : (s + 1) * REQ].astype(BF16)
    layer_out = pltpu.make_async_copy(out_v, out_o, out_sem.at[1])
    layer_out.start()
    for one in sends:
        one.wait_send()
    mass_out.wait()
    layer_out.wait()


def hand_on(mass_i, out_i, mass_o, out_o, sem):
    copies = [
        pltpu.make_async_copy(mass_i, mass_o, sem.at[0]),
        pltpu.make_async_copy(out_i, out_o, sem.at[1]),
    ]
    for one in copies:
        one.start()
    for one in copies:
        one.wait()


def body(hidden, w_query, q_gain, basis, keys, values, new_keys, new_values, block_lists, w_out):
    n_tok = keys.shape[2]
    n_local = n_tok // BLK
    new_keys, new_values = new_keys[:, :, 0], new_values[:, :, 0]
    ops = (hidden, w_query, q_gain, basis, keys, values, new_keys, new_values, block_lists, w_out.T)
    slots = lambda n, kind=F32: pltpu.VMEM((n * SLOT, HD), kind)
    landing = [pltpu.VMEM(o.shape, o.dtype) for o in ops]
    landing[4] = landing[5] = pltpu.VMEM((REQ, n_tok, HD), BF16)
    dma = lambda n: pltpu.SemaphoreType.DMA((n,))

    def run(*refs):
        refs = list(refs)
        refs[4] = refs[4].at[:, 0]
        refs[5] = refs[5].at[:, 0]
        kernel(*refs)

    shapes = (
        jax.ShapeDtypeStruct((STEPS, n_local, REQ, HEADS), F32),
        jax.ShapeDtypeStruct((STEPS, REQ, w_out.shape[1]), BF16),
    )
    raw = pl.pallas_call(
        run,
        out_shape=shapes,
        in_specs=[pl.BlockSpec(memory_space=pl.ANY)] * len(ops),
        out_specs=(pl.BlockSpec(memory_space=pl.ANY),) * 2,
        scratch_shapes=landing
        + [
            pltpu.VMEM((SLOT, block_lists.shape[3]), jnp.int32),
            pltpu.VMEM((SLOT, n_tok), F32),
            slots(STEPS),
            slots(STEPS),
            pltpu.VMEM((6 * HD, HD), BF16),
            pltpu.VMEM((w_out.shape[0], w_out.shape[1]), BF16),
            pltpu.VMEM((REQ, HD, n_tok), BF16),
            pltpu.VMEM((REQ // 2, n_tok, 2 * HD), BF16),
            pltpu.VMEM(shapes[0].shape, F32),
            pltpu.VMEM(shapes[1].shape, BF16),
        ]
        + [slots(n) for n in (16, 15, 1, 7, 16, 16)]
        + [pltpu.VMEM((REQ // 2, SLOT, HD), F32)]
        + [slots(n, BF16) for n in (16, 15, 1, 7, 16, 1, 3)]
        + [dma(n) for n in (10, 2, 30, 30, 14, 14, 30, 30, 3, 3)],
        compiler_params=pltpu.CompilerParams(
            collective_id=0, has_side_effects=True, vmem_limit_bytes=60 * 2**20
        ),
        name="decode",
    )(*ops)
    mass, layer_out = pl.pallas_call(
        hand_on,
        out_shape=shapes,
        in_specs=[pl.BlockSpec(memory_space=pl.ANY)] * 2,
        out_specs=(pl.BlockSpec(memory_space=pl.ANY),) * 2,
        scratch_shapes=[dma(2)],
        compiler_params=pltpu.CompilerParams(vmem_limit_bytes=60 * 2**20),
        name="hand_on",
    )(*raw)
    return mass.transpose(0, 2, 3, 1), layer_out


def solution(mesh):
    placed = (
        P(None, None, "ctx"),
        P("ctx", "kvh"),
        P(),
        P("kvh", None, None),
        P(None, "kvh", "ctx", None),
        P(None, "kvh", "ctx", None),
        P(None, None, "kvh", None),
        P(None, None, "kvh", None),
        P(None, None, "kvh", None),
        P("kvh", "ctx"),
    )
    return jax.shard_map(
        body,
        mesh=mesh,
        in_specs=placed,
        out_specs=(P(None, None, "kvh", "ctx"), P(None, None, "ctx")),
        check_vma=False,
    )
```

```python
import jax
import jax.numpy as jnp
from jax import lax
from jax.experimental import pallas as pl
from jax.experimental.pallas import tpu as pltpu
from jax.sharding import PartitionSpec as P

RANK = 32
BLK = 128
STEPS = 3
REQ = 4
ROWS = STEPS * REQ
SLOT = 16
STAT = 12
LOW = 16
HEADS = 16
HALF = 8
HD = 128
NONE = -1e30
FAR_FIRST = (4, 3, 5, 2, 6, 1, 7)
MESH = pl.DeviceIdType.MESH
F32 = jnp.float32
BF16 = jnp.bfloat16


def split3(x):
    hi = x.astype(BF16)
    rest = x - hi.astype(F32)
    mid = rest.astype(BF16)
    lo = (rest - mid.astype(F32)).astype(BF16)
    return hi, mid, lo


def slot(i):
    if isinstance(i, int):
        return pl.ds(i * SLOT, SLOT)
    return pl.ds(pl.multiple_of(i * SLOT, SLOT), SLOT)


def rows_of(i):
    if isinstance(i, int):
        return pl.ds(i * SLOT, ROWS)
    return pl.ds(pl.multiple_of(i * SLOT, SLOT), ROWS)


def iota(shape, dim):
    return lax.broadcasted_iota(jnp.int32, shape, dim)


def column(row):
    diag = iota((SLOT, HD), 0) == iota((SLOT, HD), 1)
    return jnp.sum(jnp.where(diag, row, 0.0), axis=1, keepdims=True)


def stat_of(x):
    return x[STAT : STAT + 1] + x[STAT + 1 : STAT + 2] + x[STAT + 2 : STAT + 3]


def with_stat(x, row):
    i = iota((SLOT, HD), 0)
    hi, mid, lo = (p.astype(F32) for p in split3(row))
    tail = jnp.where(i == STAT, hi, jnp.where(i == STAT + 1, mid, lo))
    return jnp.where(i < ROWS, x, jnp.where(i < STAT + 3, tail, 0.0)).astype(BF16)


def merge(outs, rows):
    top = rows[0]
    for one in rows[1:]:
        top = jnp.maximum(top, one)
    ws = [jnp.exp(one - top) for one in rows]
    total = sum(ws)
    inv = 1.0 / total
    res = sum(o * column(w * inv) for o, w in zip(outs, ws))
    return res, top + jnp.log(total)


def kernel(
    hid_h, wq_h, gain_h, basis_h, keys_h, vals_h, nk_h, nv_h, lists_h, wo_h,
    mass_o, out_o,
    hid_v, wq_v, gain_v, basis_v, keys_v, vals_v, nk_v, nv_v, lists_v, wo_v,
    list_rows, bias, nk_rows, nv_rows, rot, wo_t, keys_t, low_keys,
    q_part, q_rs, q_own, q_ex, q_all,
    o_wide, lse_all,
    o_part, o_rs, o_own, o_ex, o_all, x_own, x_in,
    in_sem, rs_s, rs_r, ex_s, ex_r, ag_s, ag_r, x_s, x_r,
):
    ctx = lax.axis_index("ctx")
    x = lax.axis_index("kvh")
    y = ctx // 16
    z = lax.rem(ctx // 2, 8)
    c = lax.rem(ctx, 2)
    a = z + c * (y - z)
    b = y + c * (z - y)
    mine = c * HALF + a
    theirs = (1 - c) * HALF

    def at(aa, bb, cc):
        yy = bb + c * (aa - bb)
        zz = aa + c * (bb - aa)
        return ((yy * 8 + zz) * 2 + cc, x)

    def ring_a(k):
        return lax.rem(a + k, HALF)

    def ring_b(k):
        return lax.rem(b + k, HALF)

    def dev_a(k):
        return at(ring_a(k), b, c)

    def dev_b(k):
        return at(a, ring_b(k), c)

    def cross_a(k):
        return at(ring_a(k), b, 1 - c)

    def cross_b(k):
        return at(a, ring_b(k), 1 - c)

    def dev_x(k):
        return (ctx, lax.rem(x + k, 4))

    barrier = pltpu.get_barrier_semaphore()
    partners = []
    for k in FAR_FIRST:
        partners += [dev_a(k), dev_b(k), cross_a(k), cross_b(k)]
    partners += [dev_x(2), dev_x(1), dev_x(3), cross_a(0)]
    for who in partners:
        pl.semaphore_signal(barrier, inc=1, device_id=who, device_id_type=MESH)
    pairs = (
        (hid_h, hid_v), (wq_h, wq_v), (gain_h, gain_v), (basis_h, basis_v), (lists_h, lists_v),
        (nk_h, nk_v), (nv_h, nv_v), (wo_h, wo_v), (keys_h, keys_v), (vals_h, vals_v),
    )
    fetch = [pltpu.make_async_copy(s, d, in_sem.at[i]) for i, (s, d) in enumerate(pairs)]
    for one in fetch:
        one.start()

    sends = []

    def send(src, dst, s_sem, r_sem, who):
        copy = pltpu.make_async_remote_copy(
            src_ref=src, dst_ref=dst, send_sem=s_sem, recv_sem=r_sem,
            device_id=who, device_id_type=MESH,
        )
        copy.start()
        sends.append(copy)
        return copy

    def scatter(part, into, cut, base):
        got = {}
        for k in FAR_FIRST + (0,):
            if k:
                got[k - 1] = send(
                    part.at[cut(c * HALF + ring_a(k))], into.at[cut(k - 1)],
                    rs_s.at[base + k - 1], rs_r.at[base + k - 1], dev_a(k),
                )
            got[7 + k] = send(
                part.at[cut(theirs + ring_b(k))], into.at[cut(7 + k)],
                rs_s.at[base + 7 + k], rs_r.at[base + 7 + k], cross_b(k),
            )
        return [got[i] for i in range(15)]

    def gather(buf, cut, base):
        got = {}
        for k in FAR_FIRST + (0,):
            if k:
                got[k - 1] = send(
                    buf.at[cut(mine)], buf.at[cut(mine)],
                    ag_s.at[base + k - 1], ag_r.at[base + k - 1], dev_a(k),
                )
            got[7 + k] = send(
                buf.at[cut(mine)], buf.at[cut(mine)],
                ag_s.at[base + 7 + k], ag_r.at[base + 7 + k], cross_a(k),
            )
        return [got[i] for i in range(15)]

    def exchange(own, into, cut, base):
        got = {}
        for k in FAR_FIRST:
            got[k - 1] = send(
                own.at[cut(0)], into.at[cut(k - 1)],
                ex_s.at[base + k - 1], ex_r.at[base + k - 1], dev_b(k),
            )
        return [got[i] for i in range(7)]

    fetch[0].wait()
    fetch[1].wait()
    hid = jnp.concatenate(
        [hid_v[s].astype(F32) for s in range(STEPS)] + [jnp.zeros((SLOT - ROWS, hid_v.shape[2]), F32)],
        axis=0,
    ).astype(BF16)
    for h in range(HEADS):
        q_part[slot(h)] = jnp.dot(
            hid, wq_v[:, h * HD : (h + 1) * HD], preferred_element_type=F32
        )
    pl.semaphore_wait(barrier, len(partners))

    got = scatter(q_part, q_rs, rows_of, 0)
    for one in fetch[2:9]:
        one.wait()

    list_rows[...] = jnp.full(list_rows.shape, -1, jnp.int32)
    for s in range(STEPS):
        for r in range(REQ):
            i = s * REQ + r
            list_rows[i : i + 1, :] = lists_v[s, r]
    nk_rows[...] = jnp.zeros(nk_rows.shape, F32)
    nv_rows[...] = jnp.zeros(nv_rows.shape, F32)
    for t in range(STEPS):
        one_k = nk_v[t].astype(F32)
        one_v = nv_v[t].astype(F32)
        for s in range(t, STEPS):
            i = t * SLOT + s * REQ
            nk_rows[i : i + REQ, :] = one_k
            nv_rows[i : i + REQ, :] = one_v
    n_local = keys_v.shape[1] // BLK
    first = ctx * n_local
    lists = list_rows[...]
    for blk in range(n_local):
        hit = jnp.max(jnp.where(lists == first + blk, 1.0, 0.0), axis=1, keepdims=True)
        bias[:, blk * BLK : (blk + 1) * BLK] = jnp.broadcast_to(
            jnp.where(hit > 0.5, 0.0, NONE), (SLOT, BLK)
        )
    b_hi, b_mid, b_lo = split3(basis_v[0])
    for i, piece in enumerate((b_hi, b_mid, b_lo, b_hi, b_mid, b_hi)):
        rot[i * HD : (i + 1) * HD, :] = piece
    gain = gain_v[...].reshape(1, HD)
    wo_t[...] = wo_v[...].astype(F32).T.astype(BF16)
    for r in range(REQ):
        keys_t[r] = keys_v[r].T

    total = q_part[slot(mine)]
    for k in range(15):
        got[k].wait_recv()
        total = total + q_rs[slot(k)]
    total = jnp.where(iota((SLOT, HD), 0) < ROWS, total, 0.0)
    q_own[...] = total
    got = exchange(q_own, q_ex, rows_of, 0)
    copies = (iota((HD, HD), 0) == lax.rem(iota((HD, HD), 1), RANK)).astype(F32).astype(BF16)
    for r in range(REQ):
        low_keys[r // 2, :, (r % 2) * HD : (r % 2 + 1) * HD] = jnp.dot(
            keys_v[r], copies, preferred_element_type=F32
        ).astype(BF16)
    for k in range(7):
        got[k].wait_recv()
        total = total + q_ex[slot(k)]
    total = jnp.where(iota((SLOT, HD), 0) < ROWS, total, 0.0)

    scale = HD ** (-0.5)
    norm = lax.rsqrt(jnp.mean(total * total, axis=1, keepdims=True) + 1e-06) * scale
    g_hi, g_mid, g_lo = split3(total * gain)
    turned = jnp.dot(
        jnp.concatenate([g_hi, g_hi, g_hi, g_mid, g_mid, g_lo], axis=1),
        rot[...],
        preferred_element_type=F32,
    )
    q_mine = turned * norm
    q_all[slot(mine)] = q_mine
    got = gather(q_all, rows_of, 0)
    fetch[9].wait()
    for one in got:
        one.wait_recv()

    lane16 = iota((HEADS, HD), 1)
    stat = jnp.zeros((HEADS, HD), F32)
    n_rows = STEPS * HEADS
    q_of = [
        jnp.concatenate(
            [q_all[pl.ds(s * REQ + r, HEADS, stride=SLOT), :] for s in range(STEPS)], axis=0
        )
        for r in range(REQ)
    ]
    parts_of = [split3(q) for q in q_of]
    for r in range(REQ):
        scores = jnp.dot(
            jnp.concatenate(parts_of[r], axis=0), keys_t[r], preferred_element_type=F32
        )
        scores = scores[:n_rows] + scores[n_rows : 2 * n_rows] + scores[2 * n_rows :]
        exact = jnp.concatenate(
            [
                scores[s * HEADS : (s + 1) * HEADS] + bias[s * REQ + r : s * REQ + r + 1, :]
                for s in range(STEPS)
            ],
            axis=0,
        )
        top = jnp.max(exact, axis=1, keepdims=True)
        probs = jnp.exp(exact - top)
        mass = jnp.sum(probs, axis=1, keepdims=True)
        acc = jnp.dot(probs.astype(BF16), vals_v[r], preferred_element_type=F32) / mass
        lse = top + jnp.log(mass)
        for s in range(STEPS):
            i = s * REQ + r
            rows = slice(s * HEADS, (s + 1) * HEADS)
            o_wide[pl.ds(i, HEADS, stride=SLOT), :] = acc[rows]
            stat = jnp.where(lane16 == i, lse[rows], stat)
    lane48 = iota((n_rows, HD), 1)
    for pair in range(REQ // 2):
        sides = []
        for half in range(2):
            hi, mid, lo = (p.astype(F32) for p in parts_of[2 * pair + half])
            packed = jnp.where(
                lane48 < RANK,
                hi,
                jnp.where(
                    lane48 < 2 * RANK,
                    pltpu.roll(mid, RANK, 1),
                    jnp.where(lane48 < 3 * RANK, pltpu.roll(lo, 2 * RANK, 1), 0.0),
                ),
            )
            blank = jnp.zeros((HD // 2, HD), F32)
            packed = jnp.concatenate([packed, blank[: HD // 2 - n_rows]], axis=0)
            sides.append(jnp.concatenate([blank, packed] if half else [packed, blank], axis=0).T)
        columns = jnp.concatenate(sides, axis=0).astype(BF16)
        rows = []
        for blk in range(n_local):
            part = jnp.dot(
                low_keys[pair, blk * BLK : (blk + 1) * BLK], columns, preferred_element_type=F32
            )
            peak = jnp.max(part, axis=0, keepdims=True)
            rows.append(peak + jnp.log(jnp.sum(jnp.exp(part - peak), axis=0, keepdims=True)))
        blocks = jnp.concatenate(rows, axis=0)
        peak = jnp.max(blocks, axis=0, keepdims=True)
        low_lse = peak + jnp.log(jnp.sum(jnp.exp(blocks - peak), axis=0, keepdims=True))
        lse_all[pair, :n_local] = blocks
        low_lse = jnp.broadcast_to(low_lse, (8, HD)).T
        for half in range(2):
            for s in range(STEPS):
                at_row = half * (HD // 2) + s * HEADS
                stat = jnp.where(
                    lane16 == LOW + s * REQ + 2 * pair + half,
                    low_lse[at_row : at_row + HEADS, :1],
                    stat,
                )
    for i, piece in enumerate(split3(stat)):
        o_wide[pl.ds(STAT + i, HEADS, stride=SLOT), :] = piece.astype(F32)
    o_wide[pl.ds(SLOT - 1, HEADS, stride=SLOT), :] = jnp.zeros((HEADS, HD), F32)
    o_part[...] = o_wide[...].astype(BF16)

    got = scatter(o_part, o_rs, slot, 15)
    row16 = iota((SLOT, 1), 0)
    fresh = [
        jnp.where(
            row16 >= t * REQ,
            jnp.sum(q_mine * nk_rows[slot(t)], axis=1, keepdims=True),
            NONE,
        )
        for t in range(STEPS)
    ]
    top = jnp.maximum(jnp.maximum(fresh[0], fresh[1]), fresh[2])
    new_w = [jnp.exp(f - top) for f in fresh]
    new_sum = new_w[0] + new_w[1] + new_w[2]
    new_o = sum(
        new_w[t].astype(BF16).astype(F32) * nv_rows[slot(t)] for t in range(STEPS)
    ) / new_sum
    diag = iota((SLOT, HD), 0) == iota((SLOT, HD), 1)
    new_row = jnp.sum(jnp.where(diag, top + jnp.log(new_sum), 0.0), axis=0, keepdims=True)
    new_row = jnp.where(iota((1, HD), 1) < ROWS, new_row, NONE)

    for one in got:
        one.wait_recv()
    outs = [o_wide[slot(mine)]] + [o_rs[slot(k)].astype(F32) for k in range(15)]
    res, row = merge(outs, [stat_of(p) for p in outs])
    o_own[...] = with_stat(res, row)
    got = exchange(o_own, o_ex, slot, 7)
    for one in got:
        one.wait_recv()
    outs = [o_ex[slot(k)].astype(F32) for k in range(7)]
    res, row = merge([res, new_o] + outs, [row, new_row] + [stat_of(p) for p in outs])
    o_all[slot(mine)] = with_stat(res, row)
    got = gather(o_all, slot, 15)
    for one in got:
        one.wait_recv()

    attn = jnp.concatenate([o_all[slot(h)] for h in range(HEADS)], axis=1)
    term = jnp.dot(attn, wo_t[...], preferred_element_type=F32).astype(BF16)
    cols = term.shape[1]
    x_own[:, :cols] = term
    got = [
        send(x_own, x_in.at[slot(k - 1)], x_s.at[k - 1], x_r.at[k - 1], dev_x(k))
        for k in (2, 1, 3)
    ]
    o_wide[...] = o_all[...].astype(F32)
    stat = sum(o_wide[pl.ds(STAT + i, HEADS, stride=SLOT), :] for i in range(3))
    stat = jnp.concatenate([stat, jnp.zeros((HD - HEADS, HD), F32)], axis=0).T
    for r in range(REQ):
        blocks = lse_all[r // 2]
        for s in range(STEPS):
            i = LOW + s * REQ + r
            at_lane = (r % 2) * (HD // 2) + s * HEADS
            moved = pltpu.roll(blocks, HD - at_lane, 1) if at_lane else blocks
            mass_o[s, :, r, :] = (moved - stat[i : i + 1])[:n_local, :HEADS]
    for one in got:
        one.wait_recv()
    term = term.astype(F32)
    for k in range(1, 4):
        term = term + x_in[slot(k - 1), :cols].astype(F32)
    for s in range(STEPS):
        out_o[s] = term[s * REQ : (s + 1) * REQ].astype(BF16)
    for one in sends:
        one.wait_send()


def hand_on(mass_i, out_i, mass_o, out_o, sem):
    copies = [
        pltpu.make_async_copy(mass_i, mass_o, sem.at[0]),
        pltpu.make_async_copy(out_i, out_o, sem.at[1]),
    ]
    for one in copies:
        one.start()
    for one in copies:
        one.wait()


def body(hidden, w_query, q_gain, basis, keys, values, new_keys, new_values, block_lists, w_out):
    n_tok = keys.shape[2]
    n_local = n_tok // BLK
    new_keys, new_values = new_keys[:, :, 0], new_values[:, :, 0]
    ops = (hidden, w_query, q_gain, basis, keys, values, new_keys, new_values, block_lists, w_out.T)
    ops = tuple(pltpu.with_memory_space_constraint(o, pltpu.HBM) for o in ops)
    slots = lambda n, kind=F32: pltpu.VMEM((n * SLOT, HD), kind)
    landing = [pltpu.VMEM(o.shape, o.dtype) for o in ops]
    landing[4] = landing[5] = pltpu.VMEM((REQ, n_tok, HD), BF16)
    dma = lambda n: pltpu.SemaphoreType.DMA((n,))

    def run(*refs):
        refs = list(refs)
        refs[4] = refs[4].at[:, 0]
        refs[5] = refs[5].at[:, 0]
        kernel(*refs)

    shapes = (
        jax.ShapeDtypeStruct((STEPS, n_local, REQ, HEADS), F32),
        jax.ShapeDtypeStruct((STEPS, REQ, w_out.shape[1]), BF16),
    )
    raw = pl.pallas_call(
        run,
        out_shape=shapes,
        in_specs=[pl.BlockSpec(memory_space=pl.ANY)] * len(ops),
        out_specs=(pl.BlockSpec(memory_space=pltpu.VMEM),) * 2,
        scratch_shapes=landing
        + [
            pltpu.VMEM((SLOT, block_lists.shape[3]), jnp.int32),
            pltpu.VMEM((SLOT, n_tok), F32),
            slots(STEPS),
            slots(STEPS),
            pltpu.VMEM((6 * HD, HD), BF16),
            pltpu.VMEM((w_out.shape[0], w_out.shape[1]), BF16),
            pltpu.VMEM((REQ, HD, n_tok), BF16),
            pltpu.VMEM((REQ // 2, n_tok, 2 * HD), BF16),
        ]
        + [slots(n) for n in (16, 15, 1, 7, 16, 16)]
        + [pltpu.VMEM((REQ // 2, SLOT, HD), F32)]
        + [slots(n, BF16) for n in (16, 15, 1, 7, 16, 1, 3)]
        + [dma(n) for n in (10, 30, 30, 14, 14, 30, 30, 3, 3)],
        compiler_params=pltpu.CompilerParams(
            collective_id=0, has_side_effects=True, vmem_limit_bytes=32 * 2**20
        ),
        name="decode",
    )(*ops)
    mass, layer_out = pl.pallas_call(
        hand_on,
        out_shape=shapes,
        in_specs=[pl.BlockSpec(memory_space=pl.ANY)] * 2,
        out_specs=(pl.BlockSpec(memory_space=pl.ANY),) * 2,
        scratch_shapes=[dma(2)],
        compiler_params=pltpu.CompilerParams(vmem_limit_bytes=32 * 2**20),
        name="hand_on",
    )(*raw)
    return mass.transpose(0, 2, 3, 1), layer_out


def solution(mesh):
    placed = (
        P(None, None, "ctx"),
        P("ctx", "kvh"),
        P(),
        P("kvh", None, None),
        P(None, "kvh", "ctx", None),
        P(None, "kvh", "ctx", None),
        P(None, None, "kvh", None),
        P(None, None, "kvh", None),
        P(None, None, "kvh", None),
        P("kvh", "ctx"),
    )
    return jax.shard_map(
        body,
        mesh=mesh,
        in_specs=placed,
        out_specs=(P(None, None, "kvh", "ctx"), P(None, None, "ctx")),
        check_vma=False,
    )
```

```python
import jax
import jax.numpy as jnp
from jax import lax
from jax.experimental import pallas as pl
from jax.experimental.pallas import tpu as pltpu
from jax.sharding import PartitionSpec as P

RANK = 32
BLK = 128
STEPS = 3
REQ = 4
ROWS = STEPS * REQ
SLOT = 16
STAT = 12
HEADS = 16
HALF = 8
HD = 128
NONE = -1e30
FAR_FIRST = (4, 3, 5, 2, 6, 1, 7)
NEAR = (7, 0, 6, 8, 14, 1, 5, 9, 13)
FAR = (2, 4, 10, 12, 3, 11)
NEAR_RING = (0, 6, 1, 5)
FAR_RING = (2, 4, 3)
MESH = pl.DeviceIdType.MESH
F32 = jnp.float32
BF16 = jnp.bfloat16


def split3(x):
    hi = x.astype(BF16)
    rest = x - hi.astype(F32)
    mid = rest.astype(BF16)
    lo = (rest - mid.astype(F32)).astype(BF16)
    return hi, mid, lo


def slot(i):
    if isinstance(i, int):
        return pl.ds(i * SLOT, SLOT)
    return pl.ds(pl.multiple_of(i * SLOT, SLOT), SLOT)


def rows_of(i):
    if isinstance(i, int):
        return pl.ds(i * SLOT, ROWS)
    return pl.ds(pl.multiple_of(i * SLOT, SLOT), ROWS)


def iota(shape, dim):
    return lax.broadcasted_iota(jnp.int32, shape, dim)


def column(row):
    diag = iota((SLOT, HD), 0) == iota((SLOT, HD), 1)
    return jnp.sum(jnp.where(diag, row, 0.0), axis=1, keepdims=True)


def stat_of(x):
    return x[STAT : STAT + 1] + x[STAT + 1 : STAT + 2] + x[STAT + 2 : STAT + 3]


def with_stat(x, row):
    i = iota((SLOT, HD), 0)
    hi, mid, lo = (p.astype(F32) for p in split3(row))
    tail = jnp.where(i == STAT, hi, jnp.where(i == STAT + 1, mid, lo))
    return jnp.where(i < ROWS, x, jnp.where(i < STAT + 3, tail, 0.0)).astype(BF16)


def merge(outs, rows):
    top = rows[0]
    for one in rows[1:]:
        top = jnp.maximum(top, one)
    ws = [jnp.exp(one - top) for one in rows]
    total = sum(ws)
    inv = 1.0 / total
    res = sum(o * column(w * inv) for o, w in zip(outs, ws))
    return res, top + jnp.log(total)


def kernel(
    hid_h, wq_h, gain_h, basis_h, keys_h, vals_h, nk_h, nv_h, lists_h, wo_h,
    mass_o, out_o,
    hid_v, wq_v, gain_v, basis_v, keys_v, vals_v, nk_v, nv_v, lists_v, wo_v,
    list_rows, bias, nk_rows, nv_rows, rot, wo_t, keys_t, low_keys,
    q_part, q_rs, q_own, q_ex, q_all,
    o_wide, lse_all,
    o_part, o_rs, o_own, o_ex, o_all, x_own, x_in, low_own, low_in,
    in_sem, rs_s, rs_r, ex_s, ex_r, ag_s, ag_r, x_s, x_r, low_s, low_r,
):
    ctx = lax.axis_index("ctx")
    x = lax.axis_index("kvh")
    y = ctx // 16
    z = lax.rem(ctx // 2, 8)
    c = lax.rem(ctx, 2)
    a = z + c * (y - z)
    b = y + c * (z - y)
    mine = c * HALF + a
    theirs = (1 - c) * HALF

    def at(aa, bb, cc):
        yy = bb + c * (aa - bb)
        zz = aa + c * (bb - aa)
        return ((yy * 8 + zz) * 2 + cc, x)

    def ring_a(k):
        return lax.rem(a + k, HALF)

    def ring_b(k):
        return lax.rem(b + k, HALF)

    def dev_a(k):
        return at(ring_a(k), b, c)

    def dev_b(k):
        return at(a, ring_b(k), c)

    def cross_a(k):
        return at(ring_a(k), b, 1 - c)

    def cross_b(k):
        return at(a, ring_b(k), 1 - c)

    def dev_x(k):
        return (ctx, lax.rem(x + k, 4))

    barrier = pltpu.get_barrier_semaphore()
    partners = []
    for k in FAR_FIRST:
        partners += [dev_a(k), dev_b(k), cross_a(k)]
    partners += [dev_x(2), dev_x(1), dev_x(3), cross_a(0)]
    for who in partners:
        pl.semaphore_signal(barrier, inc=1, device_id=who, device_id_type=MESH)
    pairs = (
        (hid_h, hid_v), (wq_h, wq_v), (gain_h, gain_v), (basis_h, basis_v), (lists_h, lists_v),
        (nk_h, nk_v), (nv_h, nv_v), (wo_h, wo_v), (keys_h, keys_v), (vals_h, vals_v),
    )
    fetch = [pltpu.make_async_copy(s, d, in_sem.at[i]) for i, (s, d) in enumerate(pairs)]
    for one in fetch:
        one.start()

    sends = []

    def send(src, dst, s_sem, r_sem, who):
        copy = pltpu.make_async_remote_copy(
            src_ref=src, dst_ref=dst, send_sem=s_sem, recv_sem=r_sem,
            device_id=who, device_id_type=MESH,
        )
        copy.start()
        sends.append(copy)
        return copy

    def scatter(part, into, cut, base):
        got = {}
        for k in FAR_FIRST + (0,):
            if k:
                got[k - 1] = send(
                    part.at[cut(c * HALF + ring_a(k))], into.at[cut(k - 1)],
                    rs_s.at[base + k - 1], rs_r.at[base + k - 1], dev_a(k),
                )
            got[7 + k] = send(
                part.at[cut(theirs + ring_b(k))], into.at[cut(7 + k)],
                rs_s.at[base + 7 + k], rs_r.at[base + 7 + k], cross_b(k),
            )
        return [got[i] for i in range(15)]

    def gather(buf, cut, base):
        got = {}
        for k in FAR_FIRST:
            got[k - 1] = send(
                buf.at[cut(mine)], buf.at[cut(mine)],
                ag_s.at[base + k - 1], ag_r.at[base + k - 1], dev_a(k),
            )
        for k in FAR_FIRST + (0,):
            got[7 + k] = send(
                buf.at[cut(mine)], buf.at[cut(mine)],
                ag_s.at[base + 7 + k], ag_r.at[base + 7 + k], cross_a(k),
            )
        return [got[i] for i in NEAR + FAR]

    def exchange(own, into, cut, base):
        got = {}
        for k in FAR_FIRST:
            got[k - 1] = send(
                own.at[cut(0)], into.at[cut(k - 1)],
                ex_s.at[base + k - 1], ex_r.at[base + k - 1], dev_b(k),
            )
        return [got[i] for i in range(7)]

    def low_ring(stage, dev):
        got = {}
        for k in FAR_FIRST:
            i = 7 * stage + k - 1
            got[k - 1] = send(low_own.at[stage], low_in.at[i], low_s.at[i], low_r.at[i], dev(k))
        return [got[i] for i in range(7)]

    def low_join(stage, got):
        for one in got:
            one.wait_recv()
        parts = [low_own[stage]] + [low_in[7 * stage + i] for i in range(len(got))]
        top = parts[0]
        for one in parts[1:]:
            top = jnp.maximum(top, one)
        low_own[stage + 1] = top + jnp.log(sum(jnp.exp(one - top) for one in parts))

    fetch[0].wait()
    fetch[1].wait()
    hid = jnp.concatenate(
        [hid_v[s].astype(F32) for s in range(STEPS)] + [jnp.zeros((SLOT - ROWS, hid_v.shape[2]), F32)],
        axis=0,
    ).astype(BF16)
    for h in range(HEADS):
        q_part[slot(h)] = jnp.dot(
            hid, wq_v[:, h * HD : (h + 1) * HD], preferred_element_type=F32
        )
    pl.semaphore_wait(barrier, len(partners))

    got = scatter(q_part, q_rs, rows_of, 0)
    for one in fetch[2:9]:
        one.wait()

    list_rows[...] = jnp.full(list_rows.shape, -1, jnp.int32)
    for s in range(STEPS):
        for r in range(REQ):
            i = s * REQ + r
            list_rows[i : i + 1, :] = lists_v[s, r]
    nk_rows[...] = jnp.zeros(nk_rows.shape, F32)
    nv_rows[...] = jnp.zeros(nv_rows.shape, F32)
    for t in range(STEPS):
        one_k = nk_v[t].astype(F32)
        one_v = nv_v[t].astype(F32)
        for s in range(t, STEPS):
            i = t * SLOT + s * REQ
            nk_rows[i : i + REQ, :] = one_k
            nv_rows[i : i + REQ, :] = one_v
    n_local = keys_v.shape[1] // BLK
    first = ctx * n_local
    lists = list_rows[...]
    for blk in range(n_local):
        hit = jnp.max(jnp.where(lists == first + blk, 1.0, 0.0), axis=1, keepdims=True)
        bias[:, blk * BLK : (blk + 1) * BLK] = jnp.broadcast_to(
            jnp.where(hit > 0.5, 0.0, NONE), (SLOT, BLK)
        )
    b_hi, b_mid, b_lo = split3(basis_v[0])
    for i, piece in enumerate((b_hi, b_mid, b_lo, b_hi, b_mid, b_hi)):
        rot[i * HD : (i + 1) * HD, :] = piece
    gain = gain_v[...].reshape(1, HD)
    wo_t[...] = wo_v[...].astype(F32).T.astype(BF16)
    for r in range(REQ):
        keys_t[r] = keys_v[r].T

    total = q_part[slot(mine)]
    for k in NEAR + FAR:
        got[k].wait_recv()
        total = total + q_rs[slot(k)]
    total = jnp.where(iota((SLOT, HD), 0) < ROWS, total, 0.0)
    q_own[...] = total
    got = exchange(q_own, q_ex, rows_of, 0)
    copies = (iota((HD, HD), 0) == lax.rem(iota((HD, HD), 1), RANK)).astype(F32).astype(BF16)
    for r in range(REQ):
        low_keys[r // 2, :, (r % 2) * HD : (r % 2 + 1) * HD] = jnp.dot(
            keys_v[r], copies, preferred_element_type=F32
        ).astype(BF16)
    for k in NEAR_RING + FAR_RING:
        got[k].wait_recv()
        total = total + q_ex[slot(k)]
    total = jnp.where(iota((SLOT, HD), 0) < ROWS, total, 0.0)

    scale = HD ** (-0.5)
    norm = lax.rsqrt(jnp.mean(total * total, axis=1, keepdims=True) + 1e-06) * scale
    g_hi, g_mid, g_lo = split3(total * gain)
    turned = jnp.dot(
        jnp.concatenate([g_hi, g_hi, g_hi, g_mid, g_mid, g_lo], axis=1),
        rot[...],
        preferred_element_type=F32,
    )
    q_mine = turned * norm
    q_all[slot(mine)] = q_mine
    got = gather(q_all, rows_of, 0)
    fetch[9].wait()
    for one in got:
        one.wait_recv()

    lane16 = iota((HEADS, HD), 1)
    stat = jnp.zeros((HEADS, HD), F32)
    n_rows = STEPS * HEADS
    q_of = [
        jnp.concatenate(
            [q_all[pl.ds(s * REQ + r, HEADS, stride=SLOT), :] for s in range(STEPS)], axis=0
        )
        for r in range(REQ)
    ]
    parts_of = [split3(q) for q in q_of]
    for r in range(REQ):
        scores = jnp.dot(
            jnp.concatenate(parts_of[r], axis=0), keys_t[r], preferred_element_type=F32
        )
        scores = scores[:n_rows] + scores[n_rows : 2 * n_rows] + scores[2 * n_rows :]
        exact = jnp.concatenate(
            [
                scores[s * HEADS : (s + 1) * HEADS] + bias[s * REQ + r : s * REQ + r + 1, :]
                for s in range(STEPS)
            ],
            axis=0,
        )
        top = jnp.max(exact, axis=1, keepdims=True)
        probs = jnp.exp(exact - top)
        mass = jnp.sum(probs, axis=1, keepdims=True)
        acc = jnp.dot(probs.astype(BF16), vals_v[r], preferred_element_type=F32) / mass
        lse = top + jnp.log(mass)
        for s in range(STEPS):
            i = s * REQ + r
            rows = slice(s * HEADS, (s + 1) * HEADS)
            o_wide[pl.ds(i, HEADS, stride=SLOT), :] = acc[rows]
            stat = jnp.where(lane16 == i, lse[rows], stat)
    for i, piece in enumerate(split3(stat)):
        o_wide[pl.ds(STAT + i, HEADS, stride=SLOT), :] = piece.astype(F32)
    o_wide[pl.ds(SLOT - 1, HEADS, stride=SLOT), :] = jnp.zeros((HEADS, HD), F32)
    o_part[...] = o_wide[...].astype(BF16)

    got = scatter(o_part, o_rs, slot, 15)
    lane48 = iota((n_rows, HD), 1)
    for pair in range(REQ // 2):
        sides = []
        for half in range(2):
            hi, mid, lo = (p.astype(F32) for p in parts_of[2 * pair + half])
            packed = jnp.where(
                lane48 < RANK,
                hi,
                jnp.where(
                    lane48 < 2 * RANK,
                    pltpu.roll(mid, RANK, 1),
                    jnp.where(lane48 < 3 * RANK, pltpu.roll(lo, 2 * RANK, 1), 0.0),
                ),
            )
            blank = jnp.zeros((HD // 2, HD), F32)
            packed = jnp.concatenate([packed, blank[: HD // 2 - n_rows]], axis=0)
            sides.append(jnp.concatenate([blank, packed] if half else [packed, blank], axis=0).T)
        columns = jnp.concatenate(sides, axis=0).astype(BF16)
        rows = []
        for blk in range(n_local):
            part = jnp.dot(
                low_keys[pair, blk * BLK : (blk + 1) * BLK], columns, preferred_element_type=F32
            )
            peak = jnp.max(part, axis=0, keepdims=True)
            rows.append(peak + jnp.log(jnp.sum(jnp.exp(part - peak), axis=0, keepdims=True)))
        blocks = jnp.concatenate(rows, axis=0)
        lse_all[pair, :n_local] = blocks
        peak = jnp.max(blocks, axis=0, keepdims=True)
        low_own[0, pair : pair + 1] = peak + jnp.log(
            jnp.sum(jnp.exp(blocks - peak), axis=0, keepdims=True)
        )
    low_got = low_ring(0, dev_a)
    row16 = iota((SLOT, 1), 0)
    fresh = [
        jnp.where(
            row16 >= t * REQ,
            jnp.sum(q_mine * nk_rows[slot(t)], axis=1, keepdims=True),
            NONE,
        )
        for t in range(STEPS)
    ]
    top = jnp.maximum(jnp.maximum(fresh[0], fresh[1]), fresh[2])
    new_w = [jnp.exp(f - top) for f in fresh]
    new_sum = new_w[0] + new_w[1] + new_w[2]
    new_o = sum(
        new_w[t].astype(BF16).astype(F32) * nv_rows[slot(t)] for t in range(STEPS)
    ) / new_sum
    diag = iota((SLOT, HD), 0) == iota((SLOT, HD), 1)
    new_row = jnp.sum(jnp.where(diag, top + jnp.log(new_sum), 0.0), axis=0, keepdims=True)
    new_row = jnp.where(iota((1, HD), 1) < ROWS, new_row, NONE)

    outs = [o_wide[slot(mine)]]
    for k in NEAR:
        got[k].wait_recv()
        outs.append(o_rs[slot(k)].astype(F32))
    res, row = merge(outs, [stat_of(p) for p in outs])
    outs = []
    for k in FAR:
        got[k].wait_recv()
        outs.append(o_rs[slot(k)].astype(F32))
    res, row = merge([res] + outs, [row] + [stat_of(p) for p in outs])
    o_own[...] = with_stat(res, row)
    got = exchange(o_own, o_ex, slot, 7)
    low_join(0, low_got)
    low_got = low_ring(1, dev_b)
    outs = []
    for k in NEAR_RING:
        got[k].wait_recv()
        outs.append(o_ex[slot(k)].astype(F32))
    res, row = merge([res, new_o] + outs, [row, new_row] + [stat_of(p) for p in outs])
    outs = []
    for k in FAR_RING:
        got[k].wait_recv()
        outs.append(o_ex[slot(k)].astype(F32))
    res, row = merge([res] + outs, [row] + [stat_of(p) for p in outs])
    o_all[slot(mine)] = jnp.where(iota((SLOT, HD), 0) < ROWS, res, 0.0).astype(BF16)
    got = gather(o_all, slot, 15)
    low_join(1, low_got)
    low_last = send(low_own.at[2], low_in.at[14], low_s.at[14], low_r.at[14], cross_a(0))
    for one in got:
        one.wait_recv()

    attn = jnp.concatenate([o_all[slot(h)] for h in range(HEADS)], axis=1)
    term = jnp.dot(attn, wo_t[...], preferred_element_type=F32).astype(BF16)
    cols = term.shape[1]
    x_own[:, :cols] = term
    got = [
        send(x_own, x_in.at[slot(k - 1)], x_s.at[k - 1], x_r.at[k - 1], dev_x(k))
        for k in (2, 1, 3)
    ][::-1]
    low_join(2, [low_last])
    for r in range(REQ):
        pair = r // 2
        mass = lse_all[pair] - low_own[3, pair : pair + 1]
        for s in range(STEPS):
            at_lane = (r % 2) * (HD // 2) + s * HEADS
            moved = pltpu.roll(mass, HD - at_lane, 1) if at_lane else mass
            mass_o[s, :, r, :] = moved[:n_local, :HEADS]
    for one in got:
        one.wait_recv()
    term = term.astype(F32)
    for k in range(1, 4):
        term = term + x_in[slot(k - 1), :cols].astype(F32)
    for s in range(STEPS):
        out_o[s] = term[s * REQ : (s + 1) * REQ].astype(BF16)
    for one in sends:
        one.wait_send()


def hand_on(mass_i, out_i, mass_o, out_o, sem):
    copies = [
        pltpu.make_async_copy(mass_i, mass_o, sem.at[0]),
        pltpu.make_async_copy(out_i, out_o, sem.at[1]),
    ]
    for one in copies:
        one.start()
    for one in copies:
        one.wait()


def body(hidden, w_query, q_gain, basis, keys, values, new_keys, new_values, block_lists, w_out):
    n_tok = keys.shape[2]
    n_local = n_tok // BLK
    new_keys, new_values = new_keys[:, :, 0], new_values[:, :, 0]
    ops = (hidden, w_query, q_gain, basis, keys, values, new_keys, new_values, block_lists, w_out.T)
    ops = tuple(pltpu.with_memory_space_constraint(o, pltpu.HBM) for o in ops)
    slots = lambda n, kind=F32: pltpu.VMEM((n * SLOT, HD), kind)
    landing = [pltpu.VMEM(o.shape, o.dtype) for o in ops]
    landing[4] = landing[5] = pltpu.VMEM((REQ, n_tok, HD), BF16)
    dma = lambda n: pltpu.SemaphoreType.DMA((n,))

    def run(*refs):
        refs = list(refs)
        refs[4] = refs[4].at[:, 0]
        refs[5] = refs[5].at[:, 0]
        kernel(*refs)

    shapes = (
        jax.ShapeDtypeStruct((STEPS, n_local, REQ, HEADS), F32),
        jax.ShapeDtypeStruct((STEPS, REQ, w_out.shape[1]), BF16),
    )
    raw = pl.pallas_call(
        run,
        out_shape=shapes,
        in_specs=[pl.BlockSpec(memory_space=pl.ANY)] * len(ops),
        out_specs=(pl.BlockSpec(memory_space=pltpu.VMEM),) * 2,
        scratch_shapes=landing
        + [
            pltpu.VMEM((SLOT, block_lists.shape[3]), jnp.int32),
            pltpu.VMEM((SLOT, n_tok), F32),
            slots(STEPS),
            slots(STEPS),
            pltpu.VMEM((6 * HD, HD), BF16),
            pltpu.VMEM((w_out.shape[0], w_out.shape[1]), BF16),
            pltpu.VMEM((REQ, HD, n_tok), BF16),
            pltpu.VMEM((REQ // 2, n_tok, 2 * HD), BF16),
        ]
        + [slots(n) for n in (16, 15, 1, 7, 16, 16)]
        + [pltpu.VMEM((REQ // 2, SLOT, HD), F32)]
        + [slots(n, BF16) for n in (16, 15, 1, 7, 16, 1, 3)]
        + [pltpu.VMEM((n, REQ // 2, HD), F32) for n in (4, 15)]
        + [dma(n) for n in (10, 30, 30, 14, 14, 30, 30, 3, 3, 15, 15)],
        compiler_params=pltpu.CompilerParams(
            collective_id=0, has_side_effects=True, vmem_limit_bytes=32 * 2**20
        ),
        name="decode",
    )(*ops)
    mass, layer_out = pl.pallas_call(
        hand_on,
        out_shape=shapes,
        in_specs=[pl.BlockSpec(memory_space=pl.ANY)] * 2,
        out_specs=(pl.BlockSpec(memory_space=pl.ANY),) * 2,
        scratch_shapes=[dma(2)],
        compiler_params=pltpu.CompilerParams(vmem_limit_bytes=32 * 2**20),
        name="hand_on",
    )(*raw)
    return mass.transpose(0, 2, 3, 1), layer_out


def solution(mesh):
    placed = (
        P(None, None, "ctx"),
        P("ctx", "kvh"),
        P(),
        P("kvh", None, None),
        P(None, "kvh", "ctx", None),
        P(None, "kvh", "ctx", None),
        P(None, None, "kvh", None),
        P(None, None, "kvh", None),
        P(None, None, "kvh", None),
        P("kvh", "ctx"),
    )
    return jax.shard_map(
        body,
        mesh=mesh,
        in_specs=placed,
        out_specs=(P(None, None, "kvh", "ctx"), P(None, None, "ctx")),
        check_vma=False,
    )
```

```python
import jax
import jax.numpy as jnp
from jax import lax
from jax.experimental import pallas as pl
from jax.experimental.pallas import tpu as pltpu
from jax.sharding import PartitionSpec as P

RANK = 32
BLK = 128
STEPS = 3
REQ = 4
ROWS = STEPS * REQ
SLOT = 16
STAT = 12
HEADS = 16
HALF = 8
HD = 128
NONE = -1e30
FAR_FIRST = (4, 3, 5, 2, 6, 1, 7)
NEAR = (7, 0, 6, 8, 14, 1, 5, 9, 13)
FAR = (2, 4, 10, 12, 3, 11)
NEAR_RING = (0, 6, 1, 5)
FAR_RING = (2, 4, 3)
MESH = pl.DeviceIdType.MESH
F32 = jnp.float32
BF16 = jnp.bfloat16


def split3(x):
    hi = x.astype(BF16)
    rest = x - hi.astype(F32)
    mid = rest.astype(BF16)
    lo = (rest - mid.astype(F32)).astype(BF16)
    return hi, mid, lo


def slot(i):
    if isinstance(i, int):
        return pl.ds(i * SLOT, SLOT)
    return pl.ds(pl.multiple_of(i * SLOT, SLOT), SLOT)


def rows_of(i):
    if isinstance(i, int):
        return pl.ds(i * SLOT, ROWS)
    return pl.ds(pl.multiple_of(i * SLOT, SLOT), ROWS)


def iota(shape, dim):
    return lax.broadcasted_iota(jnp.int32, shape, dim)


def column(row):
    diag = iota((SLOT, HD), 0) == iota((SLOT, HD), 1)
    return jnp.sum(jnp.where(diag, row, 0.0), axis=1, keepdims=True)


def stat_of(x):
    return x[STAT : STAT + 1] + x[STAT + 1 : STAT + 2] + x[STAT + 2 : STAT + 3]


def with_stat(x, row):
    i = iota((SLOT, HD), 0)
    hi, mid, lo = (p.astype(F32) for p in split3(row))
    tail = jnp.where(i == STAT, hi, jnp.where(i == STAT + 1, mid, lo))
    return jnp.where(i < ROWS, x, jnp.where(i < STAT + 3, tail, 0.0)).astype(BF16)


def merge(outs, rows):
    top = rows[0]
    for one in rows[1:]:
        top = jnp.maximum(top, one)
    ws = [jnp.exp(one - top) for one in rows]
    total = sum(ws)
    inv = 1.0 / total
    res = sum(o * column(w * inv) for o, w in zip(outs, ws))
    return res, top + jnp.log(total)


def kernel(
    hid_h, wq_h, gain_h, basis_h, keys_h, vals_h, nk_h, nv_h, lists_h, wo_h,
    mass_o, out_o,
    hid_v, wq_v, gain_v, basis_v, keys_v, vals_v, nk_v, nv_v, lists_v, wo_v,
    list_rows, bias, nk_rows, nv_rows, rot, wo_t, keys_t, low_keys,
    q_part, q_rs, q_own, q_ex, q_all,
    o_wide, lse_all,
    o_part, o_rs, o_own, o_ex, o_all, x_own, x_in, low_own, low_in,
    in_sem, s_sem, r_sem,
):
    ctx = lax.axis_index("ctx")
    x = lax.axis_index("kvh")
    y = ctx // 16
    z = lax.rem(ctx // 2, 8)
    c = lax.rem(ctx, 2)
    a = z + c * (y - z)
    b = y + c * (z - y)
    mine = c * HALF + a
    theirs = (1 - c) * HALF

    def at(aa, bb, cc):
        yy = bb + c * (aa - bb)
        zz = aa + c * (bb - aa)
        return ((yy * 8 + zz) * 2 + cc, x)

    def ring_a(k):
        return lax.rem(a + k, HALF)

    def ring_b(k):
        return lax.rem(b + k, HALF)

    def dev_a(k):
        return at(ring_a(k), b, c)

    def dev_b(k):
        return at(a, ring_b(k), c)

    def cross_a(k):
        return at(ring_a(k), b, 1 - c)

    def cross_b(k):
        return at(a, ring_b(k), 1 - c)

    def dev_x(k):
        return (ctx, lax.rem(x + k, 4))

    barrier = pltpu.get_barrier_semaphore()
    partners = []
    for k in FAR_FIRST:
        partners += [dev_a(k), dev_b(k), cross_a(k)]
    partners += [dev_x(2), dev_x(1), dev_x(3), cross_a(0)]
    for who in partners:
        pl.semaphore_signal(barrier, inc=1, device_id=who, device_id_type=MESH)
    pairs = (
        (hid_h, hid_v), (wq_h, wq_v), (gain_h, gain_v), (basis_h, basis_v), (lists_h, lists_v),
        (nk_h, nk_v), (nv_h, nv_v), (wo_h, wo_v), (keys_h, keys_v), (vals_h, vals_v),
    )
    fetch = [pltpu.make_async_copy(s, d, in_sem.at[i]) for i, (s, d) in enumerate(pairs)]
    for one in fetch:
        one.start()


    def send(src, dst, s_sem, r_sem, who):
        pltpu.make_async_remote_copy(
            src_ref=src, dst_ref=dst, send_sem=s_sem, recv_sem=r_sem,
            device_id=who, device_id_type=MESH,
        ).start()

    def scatter(part, into, cut, s_sem, r_sem):
        for k in FAR_FIRST + (0,):
            if k:
                send(
                    part.at[cut(c * HALF + ring_a(k))], into.at[cut(k - 1)],
                    s_sem, r_sem[k - 1 in FAR], dev_a(k),
                )
            send(
                part.at[cut(theirs + ring_b(k))], into.at[cut(7 + k)],
                s_sem, r_sem[7 + k in FAR], cross_b(k),
            )

    def gather(buf, cut, s_sem, r_sem):
        for k in FAR_FIRST:
            send(buf.at[cut(mine)], buf.at[cut(mine)], s_sem, r_sem, dev_a(k))
        for k in FAR_FIRST + (0,):
            send(buf.at[cut(mine)], buf.at[cut(mine)], s_sem, r_sem, cross_a(k))

    def exchange(own, into, cut, s_sem, r_sem):
        for k in FAR_FIRST:
            send(
                own.at[cut(0)], into.at[cut(k - 1)],
                s_sem, r_sem[k - 1 in FAR_RING], dev_b(k),
            )

    def take(ref, rows, sem):
        some = ref.at[pl.ds(0, rows)]
        pltpu.make_async_copy(some, some, sem).wait()

    def low_ring(stage, dev):
        for k in FAR_FIRST:
            send(low_own.at[stage], low_in.at[7 * stage + k - 1], s_sem.at[7], r_sem.at[11 + stage], dev(k))

    def low_join(stage, count):
        take(low_in, count, r_sem.at[11 + stage])
        parts = [low_own[stage]] + [low_in[7 * stage + i] for i in range(count)]
        top = parts[0]
        for one in parts[1:]:
            top = jnp.maximum(top, one)
        low_own[stage + 1] = top + jnp.log(sum(jnp.exp(one - top) for one in parts))

    fetch[0].wait()
    fetch[1].wait()
    hid = jnp.concatenate(
        [hid_v[s].astype(F32) for s in range(STEPS)] + [jnp.zeros((SLOT - ROWS, hid_v.shape[2]), F32)],
        axis=0,
    ).astype(BF16)
    for h in range(HEADS):
        q_part[slot(h)] = jnp.dot(
            hid, wq_v[:, h * HD : (h + 1) * HD], preferred_element_type=F32
        )
    pl.semaphore_wait(barrier, len(partners))

    scatter(q_part, q_rs, rows_of, s_sem.at[0], (r_sem.at[0], r_sem.at[1]))
    for i in (2, 3, 8):
        fetch[i].wait()

    b_hi, b_mid, b_lo = split3(basis_v[0])
    for i, piece in enumerate((b_hi, b_mid, b_lo, b_hi, b_mid, b_hi)):
        rot[i * HD : (i + 1) * HD, :] = piece
    gain = gain_v[...].reshape(1, HD)

    for r in range(REQ // 2):
        keys_t[r] = keys_v[r].T

    total = q_part[slot(mine)]
    for group, sem in ((NEAR, r_sem.at[0]), (FAR, r_sem.at[1])):
        take(q_rs, len(group) * ROWS, sem)
        total = total + sum(q_rs[slot(k)] for k in group)
    total = jnp.where(iota((SLOT, HD), 0) < ROWS, total, 0.0)
    q_own[...] = total
    exchange(q_own, q_ex, rows_of, s_sem.at[1], (r_sem.at[2], r_sem.at[3]))
    for r in range(REQ // 2, REQ):
        keys_t[r] = keys_v[r].T

    for group, sem in ((NEAR_RING, r_sem.at[2]), (FAR_RING, r_sem.at[3])):
        take(q_ex, len(group) * ROWS, sem)
        total = total + sum(q_ex[slot(k)] for k in group)
    total = jnp.where(iota((SLOT, HD), 0) < ROWS, total, 0.0)

    scale = HD ** (-0.5)
    norm = lax.rsqrt(jnp.mean(total * total, axis=1, keepdims=True) + 1e-06) * scale
    g_hi, g_mid, g_lo = split3(total * gain)
    turned = jnp.dot(
        jnp.concatenate([g_hi, g_hi, g_hi, g_mid, g_mid, g_lo], axis=1),
        rot[...],
        preferred_element_type=F32,
    )
    q_mine = turned * norm
    q_all[slot(mine)] = q_mine
    gather(q_all, rows_of, s_sem.at[2], r_sem.at[4])
    for i in (4, 5, 6, 7, 9):
        fetch[i].wait()
    list_rows[...] = jnp.full(list_rows.shape, -1, jnp.int32)
    for s in range(STEPS):
        for r in range(REQ):
            i = s * REQ + r
            list_rows[i : i + 1, :] = lists_v[s, r]
    nk_rows[...] = jnp.zeros(nk_rows.shape, F32)
    nv_rows[...] = jnp.zeros(nv_rows.shape, F32)
    for t in range(STEPS):
        one_k = nk_v[t].astype(F32)
        one_v = nv_v[t].astype(F32)
        for s in range(t, STEPS):
            i = t * SLOT + s * REQ
            nk_rows[i : i + REQ, :] = one_k
            nv_rows[i : i + REQ, :] = one_v
    n_local = keys_v.shape[1] // BLK
    first = ctx * n_local
    lists = list_rows[...]
    for blk in range(n_local):
        hit = jnp.max(jnp.where(lists == first + blk, 1.0, 0.0), axis=1, keepdims=True)
        bias[:, blk * BLK : (blk + 1) * BLK] = jnp.broadcast_to(
            jnp.where(hit > 0.5, 0.0, NONE), (SLOT, BLK)
        )
    copies = (iota((HD, HD), 0) == lax.rem(iota((HD, HD), 1), RANK)).astype(F32).astype(BF16)
    for r in range(REQ):
        low_keys[r // 2, :, (r % 2) * HD : (r % 2 + 1) * HD] = jnp.dot(
            keys_v[r], copies, preferred_element_type=F32
        ).astype(BF16)

    take(q_all, 15 * ROWS, r_sem.at[4])

    lane16 = iota((HEADS, HD), 1)
    stat = jnp.zeros((HEADS, HD), F32)
    n_rows = STEPS * HEADS
    q_of = [
        jnp.concatenate(
            [q_all[pl.ds(s * REQ + r, HEADS, stride=SLOT), :] for s in range(STEPS)], axis=0
        )
        for r in range(REQ)
    ]
    parts_of = [split3(q) for q in q_of]
    for r in range(REQ):
        scores = jnp.dot(
            jnp.concatenate(parts_of[r], axis=0), keys_t[r], preferred_element_type=F32
        )
        scores = scores[:n_rows] + scores[n_rows : 2 * n_rows] + scores[2 * n_rows :]
        exact = jnp.concatenate(
            [
                scores[s * HEADS : (s + 1) * HEADS] + bias[s * REQ + r : s * REQ + r + 1, :]
                for s in range(STEPS)
            ],
            axis=0,
        )
        top = jnp.max(exact, axis=1, keepdims=True)
        probs = jnp.exp(exact - top)
        mass = jnp.sum(probs, axis=1, keepdims=True)
        acc = jnp.dot(probs.astype(BF16), vals_v[r], preferred_element_type=F32) / mass
        lse = top + jnp.log(mass)
        for s in range(STEPS):
            i = s * REQ + r
            rows = slice(s * HEADS, (s + 1) * HEADS)
            o_wide[pl.ds(i, HEADS, stride=SLOT), :] = acc[rows]
            stat = jnp.where(lane16 == i, lse[rows], stat)
    for i, piece in enumerate(split3(stat)):
        o_wide[pl.ds(STAT + i, HEADS, stride=SLOT), :] = piece.astype(F32)
    o_wide[pl.ds(SLOT - 1, HEADS, stride=SLOT), :] = jnp.zeros((HEADS, HD), F32)
    o_part[...] = o_wide[...].astype(BF16)

    scatter(o_part, o_rs, slot, s_sem.at[3], (r_sem.at[5], r_sem.at[6]))
    lane48 = iota((n_rows, HD), 1)
    for pair in range(REQ // 2):
        sides = []
        for half in range(2):
            hi, mid, lo = (p.astype(F32) for p in parts_of[2 * pair + half])
            packed = jnp.where(
                lane48 < RANK,
                hi,
                jnp.where(
                    lane48 < 2 * RANK,
                    pltpu.roll(mid, RANK, 1),
                    jnp.where(lane48 < 3 * RANK, pltpu.roll(lo, 2 * RANK, 1), 0.0),
                ),
            )
            blank = jnp.zeros((HD // 2, HD), F32)
            packed = jnp.concatenate([packed, blank[: HD // 2 - n_rows]], axis=0)
            sides.append(jnp.concatenate([blank, packed] if half else [packed, blank], axis=0).T)
        columns = jnp.concatenate(sides, axis=0).astype(BF16)
        rows = []
        for blk in range(n_local):
            part = jnp.dot(
                low_keys[pair, blk * BLK : (blk + 1) * BLK], columns, preferred_element_type=F32
            )
            peak = jnp.max(part, axis=0, keepdims=True)
            rows.append(peak + jnp.log(jnp.sum(jnp.exp(part - peak), axis=0, keepdims=True)))
        blocks = jnp.concatenate(rows, axis=0)
        lse_all[pair, :n_local] = blocks
        peak = jnp.max(blocks, axis=0, keepdims=True)
        low_own[0, pair : pair + 1] = peak + jnp.log(
            jnp.sum(jnp.exp(blocks - peak), axis=0, keepdims=True)
        )
    low_ring(0, dev_a)
    row16 = iota((SLOT, 1), 0)
    fresh = [
        jnp.where(
            row16 >= t * REQ,
            jnp.sum(q_mine * nk_rows[slot(t)], axis=1, keepdims=True),
            NONE,
        )
        for t in range(STEPS)
    ]
    top = jnp.maximum(jnp.maximum(fresh[0], fresh[1]), fresh[2])
    new_w = [jnp.exp(f - top) for f in fresh]
    new_sum = new_w[0] + new_w[1] + new_w[2]
    new_o = sum(
        new_w[t].astype(BF16).astype(F32) * nv_rows[slot(t)] for t in range(STEPS)
    ) / new_sum
    diag = iota((SLOT, HD), 0) == iota((SLOT, HD), 1)
    new_row = jnp.sum(jnp.where(diag, top + jnp.log(new_sum), 0.0), axis=0, keepdims=True)
    new_row = jnp.where(iota((1, HD), 1) < ROWS, new_row, NONE)

    outs = [o_wide[slot(mine)]]
    take(o_rs, len(NEAR) * SLOT, r_sem.at[5])
    for k in NEAR:
        outs.append(o_rs[slot(k)].astype(F32))
    res, row = merge(outs, [stat_of(p) for p in outs])
    outs = []
    take(o_rs, len(FAR) * SLOT, r_sem.at[6])
    for k in FAR:
        outs.append(o_rs[slot(k)].astype(F32))
    res, row = merge([res] + outs, [row] + [stat_of(p) for p in outs])
    o_own[...] = with_stat(res, row)
    exchange(o_own, o_ex, slot, s_sem.at[4], (r_sem.at[7], r_sem.at[8]))
    wo_t[...] = wo_v[...].astype(F32).T.astype(BF16)
    low_join(0, 7)
    low_ring(1, dev_b)
    outs = []
    take(o_ex, len(NEAR_RING) * SLOT, r_sem.at[7])
    for k in NEAR_RING:
        outs.append(o_ex[slot(k)].astype(F32))
    res, row = merge([res, new_o] + outs, [row, new_row] + [stat_of(p) for p in outs])
    outs = []
    take(o_ex, len(FAR_RING) * SLOT, r_sem.at[8])
    for k in FAR_RING:
        outs.append(o_ex[slot(k)].astype(F32))
    res, row = merge([res] + outs, [row] + [stat_of(p) for p in outs])
    o_all[slot(mine)] = jnp.where(iota((SLOT, HD), 0) < ROWS, res, 0.0).astype(BF16)
    gather(o_all, slot, s_sem.at[5], r_sem.at[9])
    low_join(1, 7)
    send(low_own.at[2], low_in.at[14], s_sem.at[7], r_sem.at[13], cross_a(0))
    take(o_all, 15 * SLOT, r_sem.at[9])

    attn = jnp.concatenate([o_all[slot(h)] for h in range(HEADS)], axis=1)
    term = jnp.dot(attn, wo_t[...], preferred_element_type=F32).astype(BF16)
    cols = term.shape[1]
    x_own[:, :cols] = term
    for k in (2, 1, 3):
        send(x_own, x_in.at[slot(k - 1)], s_sem.at[6], r_sem.at[10], dev_x(k))
    low_join(2, 1)
    for r in range(REQ):
        pair = r // 2
        mass = lse_all[pair] - low_own[3, pair : pair + 1]
        for s in range(STEPS):
            at_lane = (r % 2) * (HD // 2) + s * HEADS
            moved = pltpu.roll(mass, HD - at_lane, 1) if at_lane else mass
            mass_o[s, :, r, :] = moved[:n_local, :HEADS]
    take(x_in, 3 * SLOT, r_sem.at[10])
    term = term.astype(F32)
    for k in range(1, 4):
        term = term + x_in[slot(k - 1), :cols].astype(F32)
    for s in range(STEPS):
        out_o[s] = term[s * REQ : (s + 1) * REQ].astype(BF16)
    for i, (ref, rows) in enumerate(
        (
            (q_rs, 15 * ROWS), (q_ex, 7 * ROWS), (q_all, 15 * ROWS), (o_rs, 15 * SLOT),
            (o_ex, 7 * SLOT), (o_all, 15 * SLOT), (x_in, 3 * SLOT), (low_in, 15),
        )
    ):
        take(ref, rows, s_sem.at[i])


def hand_on(mass_i, out_i, mass_o, out_o, sem):
    copies = [
        pltpu.make_async_copy(mass_i, mass_o, sem.at[0]),
        pltpu.make_async_copy(out_i, out_o, sem.at[1]),
    ]
    for one in copies:
        one.start()
    for one in copies:
        one.wait()


def body(hidden, w_query, q_gain, basis, keys, values, new_keys, new_values, block_lists, w_out):
    n_tok = keys.shape[2]
    n_local = n_tok // BLK
    new_keys, new_values = new_keys[:, :, 0], new_values[:, :, 0]
    ops = (hidden, w_query, q_gain, basis, keys, values, new_keys, new_values, block_lists, w_out.T)
    ops = tuple(pltpu.with_memory_space_constraint(o, pltpu.HBM) for o in ops)
    slots = lambda n, kind=F32: pltpu.VMEM((n * SLOT, HD), kind)
    landing = [pltpu.VMEM(o.shape, o.dtype) for o in ops]
    landing[4] = landing[5] = pltpu.VMEM((REQ, n_tok, HD), BF16)
    dma = lambda n: pltpu.SemaphoreType.DMA((n,))

    def run(*refs):
        refs = list(refs)
        refs[4] = refs[4].at[:, 0]
        refs[5] = refs[5].at[:, 0]
        kernel(*refs)

    shapes = (
        jax.ShapeDtypeStruct((STEPS, n_local, REQ, HEADS), F32),
        jax.ShapeDtypeStruct((STEPS, REQ, w_out.shape[1]), BF16),
    )
    raw = pl.pallas_call(
        run,
        out_shape=shapes,
        in_specs=[pl.BlockSpec(memory_space=pl.ANY)] * len(ops),
        out_specs=(pl.BlockSpec(memory_space=pltpu.VMEM),) * 2,
        scratch_shapes=landing
        + [
            pltpu.VMEM((SLOT, block_lists.shape[3]), jnp.int32),
            pltpu.VMEM((SLOT, n_tok), F32),
            slots(STEPS),
            slots(STEPS),
            pltpu.VMEM((6 * HD, HD), BF16),
            pltpu.VMEM((w_out.shape[0], w_out.shape[1]), BF16),
            pltpu.VMEM((REQ, HD, n_tok), BF16),
            pltpu.VMEM((REQ // 2, n_tok, 2 * HD), BF16),
        ]
        + [slots(n) for n in (16, 15, 1, 7, 16, 16)]
        + [pltpu.VMEM((REQ // 2, SLOT, HD), F32)]
        + [slots(n, BF16) for n in (16, 15, 1, 7, 16, 1, 3)]
        + [pltpu.VMEM((n, REQ // 2, HD), F32) for n in (4, 15)]
        + [dma(n) for n in (10, 8, 14)],
        compiler_params=pltpu.CompilerParams(
            collective_id=0, has_side_effects=True, vmem_limit_bytes=32 * 2**20
        ),
        name="decode",
    )(*ops)
    mass, layer_out = pl.pallas_call(
        hand_on,
        out_shape=shapes,
        in_specs=[pl.BlockSpec(memory_space=pl.ANY)] * 2,
        out_specs=(pl.BlockSpec(memory_space=pl.ANY),) * 2,
        scratch_shapes=[dma(2)],
        compiler_params=pltpu.CompilerParams(vmem_limit_bytes=32 * 2**20),
        name="hand_on",
    )(*raw)
    return mass.transpose(0, 2, 3, 1), layer_out


def solution(mesh):
    placed = (
        P(None, None, "ctx"),
        P("ctx", "kvh"),
        P(),
        P("kvh", None, None),
        P(None, "kvh", "ctx", None),
        P(None, "kvh", "ctx", None),
        P(None, None, "kvh", None),
        P(None, None, "kvh", None),
        P(None, None, "kvh", None),
        P("kvh", "ctx"),
    )
    return jax.shard_map(
        body,
        mesh=mesh,
        in_specs=placed,
        out_specs=(P(None, None, "kvh", "ctx"), P(None, None, "ctx")),
        check_vma=False,
    )
```

```python
import jax
import jax.numpy as jnp
from jax import lax
from jax.experimental import pallas as pl
from jax.experimental.pallas import tpu as pltpu
from jax.sharding import PartitionSpec as P

RANK = 32
BLK = 128
STEPS = 3
REQ = 4
ROWS = STEPS * REQ
SLOT = 16
STAT = 12
HEADS = 16
HALF = 8
HD = 128
NONE = -1e30
FAR_FIRST = (4, 3, 5, 2, 6, 1, 7)
NEAR = (7, 0, 6, 8, 14, 1, 5, 9, 13)
FAR = (2, 4, 10, 12, 3, 11)
NEAR_RING = (0, 6, 1, 5)
FAR_RING = (2, 4, 3)
MESH = pl.DeviceIdType.MESH
F32 = jnp.float32
BF16 = jnp.bfloat16


def split3(x):
    hi = x.astype(BF16)
    rest = x - hi.astype(F32)
    mid = rest.astype(BF16)
    lo = (rest - mid.astype(F32)).astype(BF16)
    return hi, mid, lo


def slot(i):
    if isinstance(i, int):
        return pl.ds(i * SLOT, SLOT)
    return pl.ds(pl.multiple_of(i * SLOT, SLOT), SLOT)


def rows_of(i):
    if isinstance(i, int):
        return pl.ds(i * SLOT, ROWS)
    return pl.ds(pl.multiple_of(i * SLOT, SLOT), ROWS)


def iota(shape, dim):
    return lax.broadcasted_iota(jnp.int32, shape, dim)


def column(row):
    diag = iota((SLOT, HD), 0) == iota((SLOT, HD), 1)
    return jnp.sum(jnp.where(diag, row, 0.0), axis=1, keepdims=True)


def stat_of(x):
    return x[STAT : STAT + 1] + x[STAT + 1 : STAT + 2] + x[STAT + 2 : STAT + 3]


def with_stat(x, row):
    i = iota((SLOT, HD), 0)
    hi, mid, lo = (p.astype(F32) for p in split3(row))
    tail = jnp.where(i == STAT, hi, jnp.where(i == STAT + 1, mid, lo))
    return jnp.where(i < ROWS, x, jnp.where(i < STAT + 3, tail, 0.0)).astype(BF16)


def merge(outs, rows):
    top = rows[0]
    for one in rows[1:]:
        top = jnp.maximum(top, one)
    ws = [jnp.exp(one - top) for one in rows]
    total = sum(ws)
    inv = 1.0 / total
    res = sum(o * column(w * inv) for o, w in zip(outs, ws))
    return res, top + jnp.log(total)


def kernel(
    hid_h, wq_h, gain_h, basis_h, keys_h, vals_h, nk_h, nv_h, lists_h, wo_h,
    mass_o, out_o,
    hid_v, wq_v, gain_v, basis_v, keys_v, vals_v, nk_v, nv_v, lists_v, wo_v,
    list_rows, bias, nk_rows, nv_rows, rot, wo_t, keys_t, low_keys,
    q_part, q_rs, q_own, q_ex, q_all,
    o_wide, lse_all,
    o_part, o_rs, o_own, o_ex, o_all, x_own, x_in, low_own, low_in,
    in_sem, s_sem, r_sem,
):
    ctx = lax.axis_index("ctx")
    x = lax.axis_index("kvh")
    y = ctx // 16
    z = lax.rem(ctx // 2, 8)
    c = lax.rem(ctx, 2)
    a = z + c * (y - z)
    b = y + c * (z - y)
    mine = c * HALF + a
    theirs = (1 - c) * HALF

    def at(aa, bb, cc):
        yy = bb + c * (aa - bb)
        zz = aa + c * (bb - aa)
        return ((yy * 8 + zz) * 2 + cc, x)

    def ring_a(k):
        return lax.rem(a + k, HALF)

    def ring_b(k):
        return lax.rem(b + k, HALF)

    def dev_a(k):
        return at(ring_a(k), b, c)

    def dev_b(k):
        return at(a, ring_b(k), c)

    def cross_a(k):
        return at(ring_a(k), b, 1 - c)

    def cross_b(k):
        return at(a, ring_b(k), 1 - c)

    def dev_x(k):
        return (ctx, lax.rem(x + k, 4))

    pairs = (
        (hid_h, hid_v), (wq_h, wq_v), (gain_h, gain_v), (basis_h, basis_v), (lists_h, lists_v),
        (nk_h, nk_v), (nv_h, nv_v), (wo_h, wo_v), (keys_h, keys_v), (vals_h, vals_v),
    )
    fetch = [pltpu.make_async_copy(s, d, in_sem.at[i]) for i, (s, d) in enumerate(pairs)]
    for one in fetch[:2]:
        one.start()
    barrier = pltpu.get_barrier_semaphore()
    partners = []
    for k in FAR_FIRST:
        partners += [dev_a(k), dev_b(k), cross_a(k)]
    partners += [dev_x(2), dev_x(1), dev_x(3), cross_a(0)]
    for who in partners:
        pl.semaphore_signal(barrier, inc=1, device_id=who, device_id_type=MESH)
    for one in fetch[2:]:
        one.start()


    def send(src, dst, s_sem, r_sem, who):
        pltpu.make_async_remote_copy(
            src_ref=src, dst_ref=dst, send_sem=s_sem, recv_sem=r_sem,
            device_id=who, device_id_type=MESH,
        ).start()

    def scatter(part, into, cut, s_sem, r_sem):
        for k in FAR_FIRST + (0,):
            if k:
                send(
                    part.at[cut(c * HALF + ring_a(k))], into.at[cut(k - 1)],
                    s_sem, r_sem[k - 1 in FAR], dev_a(k),
                )
            send(
                part.at[cut(theirs + ring_b(k))], into.at[cut(7 + k)],
                s_sem, r_sem[7 + k in FAR], cross_b(k),
            )

    def gather(buf, cut, s_sem, r_sem):
        for k in FAR_FIRST:
            send(buf.at[cut(mine)], buf.at[cut(mine)], s_sem, r_sem, dev_a(k))
        for k in FAR_FIRST + (0,):
            send(buf.at[cut(mine)], buf.at[cut(mine)], s_sem, r_sem, cross_a(k))

    def exchange(own, into, cut, s_sem, r_sem):
        for k in FAR_FIRST:
            send(
                own.at[cut(0)], into.at[cut(k - 1)],
                s_sem, r_sem[k - 1 in FAR_RING], dev_b(k),
            )

    def take(ref, rows, sem):
        some = ref.at[pl.ds(0, rows)]
        pltpu.make_async_copy(some, some, sem).wait()

    def low_ring(stage, dev):
        for k in FAR_FIRST:
            send(low_own.at[stage], low_in.at[7 * stage + k - 1], s_sem.at[7], r_sem.at[11 + stage], dev(k))

    def low_join(stage, count):
        take(low_in, count, r_sem.at[11 + stage])
        parts = [low_own[stage]] + [low_in[7 * stage + i] for i in range(count)]
        top = parts[0]
        for one in parts[1:]:
            top = jnp.maximum(top, one)
        low_own[stage + 1] = top + jnp.log(sum(jnp.exp(one - top) for one in parts))

    fetch[0].wait()
    fetch[1].wait()
    hid = jnp.concatenate(
        [hid_v[s].astype(F32) for s in range(STEPS)] + [jnp.zeros((SLOT - ROWS, hid_v.shape[2]), F32)],
        axis=0,
    ).astype(BF16)
    for h in range(HEADS):
        q_part[slot(h)] = jnp.dot(
            hid, wq_v[:, h * HD : (h + 1) * HD], preferred_element_type=F32
        )
    pl.semaphore_wait(barrier, len(partners))

    scatter(q_part, q_rs, rows_of, s_sem.at[0], (r_sem.at[0], r_sem.at[1]))
    for i in (2, 3, 8):
        fetch[i].wait()

    b_hi, b_mid, b_lo = split3(basis_v[0])
    for i, piece in enumerate((b_hi, b_mid, b_lo, b_hi, b_mid, b_hi)):
        rot[i * HD : (i + 1) * HD, :] = piece
    gain = gain_v[...].reshape(1, HD)

    for r in range(REQ // 2):
        keys_t[r] = keys_v[r].T

    total = q_part[slot(mine)]
    for group, sem in ((NEAR, r_sem.at[0]), (FAR, r_sem.at[1])):
        take(q_rs, len(group) * ROWS, sem)
        total = total + sum(q_rs[slot(k)] for k in group)
    total = jnp.where(iota((SLOT, HD), 0) < ROWS, total, 0.0)
    q_own[...] = total
    exchange(q_own, q_ex, rows_of, s_sem.at[1], (r_sem.at[2], r_sem.at[3]))
    for r in range(REQ // 2, REQ):
        keys_t[r] = keys_v[r].T

    for group, sem in ((NEAR_RING, r_sem.at[2]), (FAR_RING, r_sem.at[3])):
        take(q_ex, len(group) * ROWS, sem)
        total = total + sum(q_ex[slot(k)] for k in group)
    total = jnp.where(iota((SLOT, HD), 0) < ROWS, total, 0.0)

    scale = HD ** (-0.5)
    norm = lax.rsqrt(jnp.mean(total * total, axis=1, keepdims=True) + 1e-06) * scale
    g_hi, g_mid, g_lo = split3(total * gain)
    turned = jnp.dot(
        jnp.concatenate([g_hi, g_hi, g_hi, g_mid, g_mid, g_lo], axis=1),
        rot[...],
        preferred_element_type=F32,
    )
    q_mine = turned * norm
    q_all[slot(mine)] = q_mine
    gather(q_all, rows_of, s_sem.at[2], r_sem.at[4])
    for i in (4, 5, 6, 7, 9):
        fetch[i].wait()
    list_rows[...] = jnp.full(list_rows.shape, -1, jnp.int32)
    for s in range(STEPS):
        for r in range(REQ):
            i = s * REQ + r
            list_rows[i : i + 1, :] = lists_v[s, r]
    nk_rows[...] = jnp.zeros(nk_rows.shape, F32)
    nv_rows[...] = jnp.zeros(nv_rows.shape, F32)
    for t in range(STEPS):
        one_k = nk_v[t].astype(F32)
        one_v = nv_v[t].astype(F32)
        for s in range(t, STEPS):
            i = t * SLOT + s * REQ
            nk_rows[i : i + REQ, :] = one_k
            nv_rows[i : i + REQ, :] = one_v
    n_local = keys_v.shape[1] // BLK
    first = ctx * n_local
    lists = list_rows[...]
    for blk in range(n_local):
        hit = jnp.max(jnp.where(lists == first + blk, 1.0, 0.0), axis=1, keepdims=True)
        bias[:, blk * BLK : (blk + 1) * BLK] = jnp.broadcast_to(
            jnp.where(hit > 0.5, 0.0, NONE), (SLOT, BLK)
        )
    take(q_all, 15 * ROWS, r_sem.at[4])

    lane16 = iota((HEADS, HD), 1)
    stat = jnp.zeros((HEADS, HD), F32)
    n_rows = STEPS * HEADS
    q_of = [
        jnp.concatenate(
            [q_all[pl.ds(s * REQ + r, HEADS, stride=SLOT), :] for s in range(STEPS)], axis=0
        )
        for r in range(REQ)
    ]
    parts_of = [split3(q) for q in q_of]
    exact_of = []
    for r in range(REQ):
        scores = jnp.dot(
            jnp.concatenate(parts_of[r], axis=0), keys_t[r], preferred_element_type=F32
        )
        scores = scores[:n_rows] + scores[n_rows : 2 * n_rows] + scores[2 * n_rows :]
        exact_of.append(
            jnp.concatenate(
                [
                    scores[s * HEADS : (s + 1) * HEADS] + bias[s * REQ + r : s * REQ + r + 1, :]
                    for s in range(STEPS)
                ],
                axis=0,
            )
        )
    soft_of = []
    for exact in exact_of:
        top = jnp.max(exact, axis=1, keepdims=True)
        probs = jnp.exp(exact - top)
        soft_of.append((top, probs.astype(BF16), jnp.sum(probs, axis=1, keepdims=True)))
    for r, (top, probs, mass) in enumerate(soft_of):
        acc = jnp.dot(probs, vals_v[r], preferred_element_type=F32) / mass
        lse = top + jnp.log(mass)
        for s in range(STEPS):
            i = s * REQ + r
            rows = slice(s * HEADS, (s + 1) * HEADS)
            o_wide[pl.ds(i, HEADS, stride=SLOT), :] = acc[rows]
            stat = jnp.where(lane16 == i, lse[rows], stat)
    for i, piece in enumerate(split3(stat)):
        o_wide[pl.ds(STAT + i, HEADS, stride=SLOT), :] = piece.astype(F32)
    o_wide[pl.ds(SLOT - 1, HEADS, stride=SLOT), :] = jnp.zeros((HEADS, HD), F32)
    o_part[...] = o_wide[...].astype(BF16)

    scatter(o_part, o_rs, slot, s_sem.at[3], (r_sem.at[5], r_sem.at[6]))
    copies = (iota((HD, HD), 0) == lax.rem(iota((HD, HD), 1), RANK)).astype(F32).astype(BF16)
    for r in range(REQ):
        low_keys[r // 2, :, (r % 2) * HD : (r % 2 + 1) * HD] = jnp.dot(
            keys_v[r], copies, preferred_element_type=F32
        ).astype(BF16)
    lane48 = iota((n_rows, HD), 1)
    for pair in range(REQ // 2):
        sides = []
        for half in range(2):
            hi, mid, lo = (p.astype(F32) for p in parts_of[2 * pair + half])
            packed = jnp.where(
                lane48 < RANK,
                hi,
                jnp.where(
                    lane48 < 2 * RANK,
                    pltpu.roll(mid, RANK, 1),
                    jnp.where(lane48 < 3 * RANK, pltpu.roll(lo, 2 * RANK, 1), 0.0),
                ),
            )
            blank = jnp.zeros((HD // 2, HD), F32)
            packed = jnp.concatenate([packed, blank[: HD // 2 - n_rows]], axis=0)
            sides.append(jnp.concatenate([blank, packed] if half else [packed, blank], axis=0).T)
        columns = jnp.concatenate(sides, axis=0).astype(BF16)
        rows = []
        for blk in range(n_local):
            part = jnp.dot(
                low_keys[pair, blk * BLK : (blk + 1) * BLK], columns, preferred_element_type=F32
            )
            peak = jnp.max(part, axis=0, keepdims=True)
            rows.append(peak + jnp.log(jnp.sum(jnp.exp(part - peak), axis=0, keepdims=True)))
        blocks = jnp.concatenate(rows, axis=0)
        lse_all[pair, :n_local] = blocks
        peak = jnp.max(blocks, axis=0, keepdims=True)
        low_own[0, pair : pair + 1] = peak + jnp.log(
            jnp.sum(jnp.exp(blocks - peak), axis=0, keepdims=True)
        )
    low_ring(0, dev_a)
    row16 = iota((SLOT, 1), 0)
    fresh = [
        jnp.where(
            row16 >= t * REQ,
            jnp.sum(q_mine * nk_rows[slot(t)], axis=1, keepdims=True),
            NONE,
        )
        for t in range(STEPS)
    ]
    top = jnp.maximum(jnp.maximum(fresh[0], fresh[1]), fresh[2])
    new_w = [jnp.exp(f - top) for f in fresh]
    new_sum = new_w[0] + new_w[1] + new_w[2]
    new_o = sum(
        new_w[t].astype(BF16).astype(F32) * nv_rows[slot(t)] for t in range(STEPS)
    ) / new_sum
    diag = iota((SLOT, HD), 0) == iota((SLOT, HD), 1)
    new_row = jnp.sum(jnp.where(diag, top + jnp.log(new_sum), 0.0), axis=0, keepdims=True)
    new_row = jnp.where(iota((1, HD), 1) < ROWS, new_row, NONE)

    outs = [o_wide[slot(mine)]]
    take(o_rs, len(NEAR) * SLOT, r_sem.at[5])
    for k in NEAR:
        outs.append(o_rs[slot(k)].astype(F32))
    res, row = merge(outs, [stat_of(p) for p in outs])
    outs = []
    take(o_rs, len(FAR) * SLOT, r_sem.at[6])
    for k in FAR:
        outs.append(o_rs[slot(k)].astype(F32))
    res, row = merge([res] + outs, [row] + [stat_of(p) for p in outs])
    o_own[...] = with_stat(res, row)
    exchange(o_own, o_ex, slot, s_sem.at[4], (r_sem.at[7], r_sem.at[8]))
    wo_t[...] = wo_v[...].astype(F32).T.astype(BF16)
    low_join(0, 7)
    low_ring(1, dev_b)
    outs = []
    take(o_ex, len(NEAR_RING) * SLOT, r_sem.at[7])
    for k in NEAR_RING:
        outs.append(o_ex[slot(k)].astype(F32))
    res, row = merge([res, new_o] + outs, [row, new_row] + [stat_of(p) for p in outs])
    outs = []
    take(o_ex, len(FAR_RING) * SLOT, r_sem.at[8])
    for k in FAR_RING:
        outs.append(o_ex[slot(k)].astype(F32))
    res, row = merge([res] + outs, [row] + [stat_of(p) for p in outs])
    o_all[slot(mine)] = jnp.where(iota((SLOT, HD), 0) < ROWS, res, 0.0).astype(BF16)
    gather(o_all, slot, s_sem.at[5], r_sem.at[9])
    low_join(1, 7)
    send(low_own.at[2], low_in.at[14], s_sem.at[7], r_sem.at[13], cross_a(0))
    take(o_all, 15 * SLOT, r_sem.at[9])

    terms = []
    for g in range(0, HEADS, 4):
        attn = jnp.concatenate([o_all[slot(h)] for h in range(g, g + 4)], axis=1)
        terms.append(
            jnp.dot(attn, wo_t[g * HD : (g + 4) * HD, :], preferred_element_type=F32)
        )
    term = ((terms[0] + terms[1]) + (terms[2] + terms[3])).astype(BF16)
    cols = term.shape[1]
    x_own[:, :cols] = term
    for k in (2, 1, 3):
        send(x_own, x_in.at[slot(k - 1)], s_sem.at[6], r_sem.at[10], dev_x(k))
    low_join(2, 1)
    for r in range(REQ):
        pair = r // 2
        mass = lse_all[pair] - low_own[3, pair : pair + 1]
        for s in range(STEPS):
            at_lane = (r % 2) * (HD // 2) + s * HEADS
            moved = pltpu.roll(mass, HD - at_lane, 1) if at_lane else mass
            mass_o[s, :, r, :] = moved[:n_local, :HEADS]
    take(x_in, 3 * SLOT, r_sem.at[10])
    term = term.astype(F32)
    for k in range(1, 4):
        term = term + x_in[slot(k - 1), :cols].astype(F32)
    for s in range(STEPS):
        out_o[s] = term[s * REQ : (s + 1) * REQ].astype(BF16)
    for i, (ref, rows) in enumerate(
        (
            (q_rs, 15 * ROWS), (q_ex, 7 * ROWS), (q_all, 15 * ROWS), (o_rs, 15 * SLOT),
            (o_ex, 7 * SLOT), (o_all, 15 * SLOT), (x_in, 3 * SLOT), (low_in, 15),
        )
    ):
        take(ref, rows, s_sem.at[i])


def hand_on(mass_i, out_i, mass_o, out_o, sem):
    copies = [
        pltpu.make_async_copy(mass_i, mass_o, sem.at[0]),
        pltpu.make_async_copy(out_i, out_o, sem.at[1]),
    ]
    for one in copies:
        one.start()
    for one in copies:
        one.wait()


def body(hidden, w_query, q_gain, basis, keys, values, new_keys, new_values, block_lists, w_out):
    n_tok = keys.shape[2]
    n_local = n_tok // BLK
    new_keys, new_values = new_keys[:, :, 0], new_values[:, :, 0]
    ops = (hidden, w_query, q_gain, basis, keys, values, new_keys, new_values, block_lists, w_out.T)
    ops = tuple(pltpu.with_memory_space_constraint(o, pltpu.HBM) for o in ops)
    slots = lambda n, kind=F32: pltpu.VMEM((n * SLOT, HD), kind)
    landing = [pltpu.VMEM(o.shape, o.dtype) for o in ops]
    landing[4] = landing[5] = pltpu.VMEM((REQ, n_tok, HD), BF16)
    dma = lambda n: pltpu.SemaphoreType.DMA((n,))

    def run(*refs):
        refs = list(refs)
        refs[4] = refs[4].at[:, 0]
        refs[5] = refs[5].at[:, 0]
        kernel(*refs)

    shapes = (
        jax.ShapeDtypeStruct((STEPS, n_local, REQ, HEADS), F32),
        jax.ShapeDtypeStruct((STEPS, REQ, w_out.shape[1]), BF16),
    )
    raw = pl.pallas_call(
        run,
        out_shape=shapes,
        in_specs=[pl.BlockSpec(memory_space=pl.ANY)] * len(ops),
        out_specs=(pl.BlockSpec(memory_space=pltpu.VMEM),) * 2,
        scratch_shapes=landing
        + [
            pltpu.VMEM((SLOT, block_lists.shape[3]), jnp.int32),
            pltpu.VMEM((SLOT, n_tok), F32),
            slots(STEPS),
            slots(STEPS),
            pltpu.VMEM((6 * HD, HD), BF16),
            pltpu.VMEM((w_out.shape[0], w_out.shape[1]), BF16),
            pltpu.VMEM((REQ, HD, n_tok), BF16),
            pltpu.VMEM((REQ // 2, n_tok, 2 * HD), BF16),
        ]
        + [slots(n) for n in (16, 15, 1, 7, 16, 16)]
        + [pltpu.VMEM((REQ // 2, SLOT, HD), F32)]
        + [slots(n, BF16) for n in (16, 15, 1, 7, 16, 1, 3)]
        + [pltpu.VMEM((n, REQ // 2, HD), F32) for n in (4, 15)]
        + [dma(n) for n in (10, 8, 14)],
        compiler_params=pltpu.CompilerParams(
            collective_id=0, has_side_effects=True, vmem_limit_bytes=32 * 2**20
        ),
        name="decode",
    )(*ops)
    mass, layer_out = pl.pallas_call(
        hand_on,
        out_shape=shapes,
        in_specs=[pl.BlockSpec(memory_space=pl.ANY)] * 2,
        out_specs=(pl.BlockSpec(memory_space=pl.ANY),) * 2,
        scratch_shapes=[dma(2)],
        compiler_params=pltpu.CompilerParams(vmem_limit_bytes=32 * 2**20),
        name="hand_on",
    )(*raw)
    return mass.transpose(0, 2, 3, 1), layer_out


def solution(mesh):
    placed = (
        P(None, None, "ctx"),
        P("ctx", "kvh"),
        P(),
        P("kvh", None, None),
        P(None, "kvh", "ctx", None),
        P(None, "kvh", "ctx", None),
        P(None, None, "kvh", None),
        P(None, None, "kvh", None),
        P(None, None, "kvh", None),
        P("kvh", "ctx"),
    )
    return jax.shard_map(
        body,
        mesh=mesh,
        in_specs=placed,
        out_specs=(P(None, None, "kvh", "ctx"), P(None, None, "ctx")),
        check_vma=False,
    )
```

```python
import jax
import jax.numpy as jnp
from jax import lax
from jax.experimental import pallas as pl
from jax.experimental.pallas import tpu as pltpu
from jax.sharding import PartitionSpec as P

RANK = 32
BLK = 128
STEPS = 3
REQ = 4
ROWS = STEPS * REQ
SLOT = 16
STAT = 12
HEADS = 16
HALF = 8
HD = 128
NONE = -1e30
FAR_FIRST = (4, 3, 5, 2, 6, 1, 7)
NEAR = (7, 0, 6, 8, 14, 1, 5, 9, 13)
FAR = (2, 4, 10, 12, 3, 11)
NEAR_RING = (0, 6, 1, 5)
FAR_RING = (2, 4, 3)
MESH = pl.DeviceIdType.MESH
F32 = jnp.float32
BF16 = jnp.bfloat16


def split3(x):
    hi = x.astype(BF16)
    rest = x - hi.astype(F32)
    mid = rest.astype(BF16)
    lo = (rest - mid.astype(F32)).astype(BF16)
    return hi, mid, lo


def slot(i):
    if isinstance(i, int):
        return pl.ds(i * SLOT, SLOT)
    return pl.ds(pl.multiple_of(i * SLOT, SLOT), SLOT)


def rows_of(i):
    if isinstance(i, int):
        return pl.ds(i * SLOT, ROWS)
    return pl.ds(pl.multiple_of(i * SLOT, SLOT), ROWS)


def iota(shape, dim):
    return lax.broadcasted_iota(jnp.int32, shape, dim)


def column(row):
    diag = iota((SLOT, HD), 0) == iota((SLOT, HD), 1)
    return jnp.sum(jnp.where(diag, row, 0.0), axis=1, keepdims=True)


def stat_of(x):
    return x[STAT : STAT + 1] + x[STAT + 1 : STAT + 2] + x[STAT + 2 : STAT + 3]


def with_stat(x, row):
    i = iota((SLOT, HD), 0)
    hi, mid, lo = (p.astype(F32) for p in split3(row))
    tail = jnp.where(i == STAT, hi, jnp.where(i == STAT + 1, mid, lo))
    return jnp.where(i < ROWS, x, jnp.where(i < STAT + 3, tail, 0.0)).astype(BF16)


def merge(outs, rows):
    top = rows[0]
    for one in rows[1:]:
        top = jnp.maximum(top, one)
    ws = [jnp.exp(one - top) for one in rows]
    total = sum(ws)
    inv = 1.0 / total
    res = sum(o * column(w * inv) for o, w in zip(outs, ws))
    return res, top + jnp.log(total)


def kernel(
    hid_h, wq_h, gain_h, basis_h, keys_h, vals_h, nk_h, nv_h, lists_h, wo_h,
    mass_o, out_o,
    hid_v, wq_v, gain_v, basis_v, keys_v, vals_v, nk_v, nv_v, lists_v, wo_v,
    list_rows, bias, nk_rows, nv_rows, rot, wo_t, keys_t, low_keys,
    q_part, q_rs, q_own, q_ex, q_all,
    o_wide, lse_all,
    o_part, o_rs, o_own, o_ex, o_all, x_own, x_in, low_own, low_in,
    in_sem, s_sem, r_sem,
):
    ctx = lax.axis_index("ctx")
    x = lax.axis_index("kvh")
    y = ctx // 16
    z = lax.rem(ctx // 2, 8)
    c = lax.rem(ctx, 2)
    a = z + c * (y - z)
    b = y + c * (z - y)
    mine = c * HALF + a
    theirs = (1 - c) * HALF

    def at(aa, bb, cc):
        yy = bb + c * (aa - bb)
        zz = aa + c * (bb - aa)
        return ((yy * 8 + zz) * 2 + cc, x)

    def ring_a(k):
        return lax.rem(a + k, HALF)

    def ring_b(k):
        return lax.rem(b + k, HALF)

    def dev_a(k):
        return at(ring_a(k), b, c)

    def dev_b(k):
        return at(a, ring_b(k), c)

    def cross_a(k):
        return at(ring_a(k), b, 1 - c)

    def cross_b(k):
        return at(a, ring_b(k), 1 - c)

    def dev_x(k):
        return (ctx, lax.rem(x + k, 4))

    pairs = (
        (hid_h, hid_v), (wq_h, wq_v), (gain_h, gain_v), (basis_h, basis_v), (lists_h, lists_v),
        (nk_h, nk_v), (nv_h, nv_v), (wo_h, wo_v), (keys_h, keys_v), (vals_h, vals_v),
    )
    fetch = [pltpu.make_async_copy(s, d, in_sem.at[i]) for i, (s, d) in enumerate(pairs)]
    for one in fetch[:2]:
        one.start()
    barrier = pltpu.get_barrier_semaphore()
    partners = []
    for k in FAR_FIRST:
        partners += [dev_a(k), cross_a(k), dev_b(k)]
        partners += {5: [dev_x(2)], 6: [dev_x(1), dev_x(3)]}.get(k, [])
    partners.append(cross_a(0))
    for who in partners:
        pl.semaphore_signal(barrier, inc=1, device_id=who, device_id_type=MESH)
    for one in fetch[2:]:
        one.start()


    def send(src, dst, s_sem, r_sem, who):
        pltpu.make_async_remote_copy(
            src_ref=src, dst_ref=dst, send_sem=s_sem, recv_sem=r_sem,
            device_id=who, device_id_type=MESH,
        ).start()

    def scatter(part, into, cut, s_sem, r_sem):
        for k in FAR_FIRST + (0,):
            if k:
                send(
                    part.at[cut(c * HALF + ring_a(k))], into.at[cut(k - 1)],
                    s_sem, r_sem[k - 1 in FAR], dev_a(k),
                )
            send(
                part.at[cut(theirs + ring_b(k))], into.at[cut(7 + k)],
                s_sem, r_sem[7 + k in FAR], cross_b(k),
            )

    def gather(buf, cut, s_sem, r_sem):
        for k in FAR_FIRST:
            send(buf.at[cut(mine)], buf.at[cut(mine)], s_sem, r_sem, dev_a(k))
        for k in FAR_FIRST + (0,):
            send(buf.at[cut(mine)], buf.at[cut(mine)], s_sem, r_sem, cross_a(k))

    def exchange(own, into, cut, s_sem, r_sem):
        for k in FAR_FIRST:
            send(
                own.at[cut(0)], into.at[cut(k - 1)],
                s_sem, r_sem[k - 1 in FAR_RING], dev_b(k),
            )

    def take(ref, rows, sem):
        some = ref.at[pl.ds(0, rows)]
        pltpu.make_async_copy(some, some, sem).wait()

    def low_ring(stage, dev):
        for k in FAR_FIRST:
            send(low_own.at[stage], low_in.at[7 * stage + k - 1], s_sem.at[7], r_sem.at[11 + stage], dev(k))

    def low_join(stage, count):
        take(low_in, count, r_sem.at[11 + stage])
        parts = [low_own[stage]] + [low_in[7 * stage + i] for i in range(count)]
        top = parts[0]
        for one in parts[1:]:
            top = jnp.maximum(top, one)
        low_own[stage + 1] = top + jnp.log(sum(jnp.exp(one - top) for one in parts))

    fetch[0].wait()
    fetch[1].wait()
    hid = jnp.concatenate(
        [hid_v[s].astype(F32) for s in range(STEPS)] + [jnp.zeros((SLOT - ROWS, hid_v.shape[2]), F32)],
        axis=0,
    ).astype(BF16)
    for h in range(HEADS):
        q_part[slot(h)] = jnp.dot(
            hid, wq_v[:, h * HD : (h + 1) * HD], preferred_element_type=F32
        )
    pl.semaphore_wait(barrier, len(partners))

    scatter(q_part, q_rs, rows_of, s_sem.at[0], (r_sem.at[0], r_sem.at[1]))
    for i in (2, 3, 8):
        fetch[i].wait()

    b_hi, b_mid, b_lo = split3(basis_v[0])
    for i, piece in enumerate((b_hi, b_mid, b_lo, b_hi, b_mid, b_hi)):
        rot[i * HD : (i + 1) * HD, :] = piece
    gain = gain_v[...].reshape(1, HD)

    for r in range(REQ // 2):
        keys_t[r] = keys_v[r].T

    total = q_part[slot(mine)]
    for group, sem in ((NEAR, r_sem.at[0]), (FAR, r_sem.at[1])):
        take(q_rs, len(group) * ROWS, sem)
        total = total + sum(q_rs[slot(k)] for k in group)
    total = jnp.where(iota((SLOT, HD), 0) < ROWS, total, 0.0)
    q_own[...] = total
    exchange(q_own, q_ex, rows_of, s_sem.at[1], (r_sem.at[2], r_sem.at[3]))
    for r in range(REQ // 2, REQ):
        keys_t[r] = keys_v[r].T

    for group, sem in ((NEAR_RING, r_sem.at[2]), (FAR_RING, r_sem.at[3])):
        take(q_ex, len(group) * ROWS, sem)
        total = total + sum(q_ex[slot(k)] for k in group)
    total = jnp.where(iota((SLOT, HD), 0) < ROWS, total, 0.0)

    scale = HD ** (-0.5)
    norm = lax.rsqrt(jnp.mean(total * total, axis=1, keepdims=True) + 1e-06) * scale
    g_hi, g_mid, g_lo = split3(total * gain)
    turned = jnp.dot(
        jnp.concatenate([g_hi, g_hi, g_hi, g_mid, g_mid, g_lo], axis=1),
        rot[...],
        preferred_element_type=F32,
    )
    q_mine = turned * norm
    q_all[slot(mine)] = q_mine
    gather(q_all, rows_of, s_sem.at[2], r_sem.at[4])
    for i in (4, 5, 6, 7, 9):
        fetch[i].wait()
    list_rows[...] = jnp.full(list_rows.shape, -1, jnp.int32)
    for s in range(STEPS):
        for r in range(REQ):
            i = s * REQ + r
            list_rows[i : i + 1, :] = lists_v[s, r]
    nk_rows[...] = jnp.zeros(nk_rows.shape, F32)
    nv_rows[...] = jnp.zeros(nv_rows.shape, F32)
    for t in range(STEPS):
        one_k = nk_v[t].astype(F32)
        one_v = nv_v[t].astype(F32)
        for s in range(t, STEPS):
            i = t * SLOT + s * REQ
            nk_rows[i : i + REQ, :] = one_k
            nv_rows[i : i + REQ, :] = one_v
    n_local = keys_v.shape[1] // BLK
    first = ctx * n_local
    lists = list_rows[...]
    for blk in range(n_local):
        hit = jnp.max(jnp.where(lists == first + blk, 1.0, 0.0), axis=1, keepdims=True)
        bias[:, blk * BLK : (blk + 1) * BLK] = jnp.broadcast_to(
            jnp.where(hit > 0.5, 0.0, NONE), (SLOT, BLK)
        )
    take(q_all, 15 * ROWS, r_sem.at[4])

    lane16 = iota((HEADS, HD), 1)
    stat = jnp.zeros((HEADS, HD), F32)
    n_rows = STEPS * HEADS
    q_of = [
        jnp.concatenate(
            [q_all[pl.ds(s * REQ + r, HEADS, stride=SLOT), :] for s in range(STEPS)], axis=0
        )
        for r in range(REQ)
    ]
    parts_of = [split3(q) for q in q_of]
    exact_of = []
    for r in range(REQ):
        scores = jnp.dot(
            jnp.concatenate(parts_of[r], axis=0), keys_t[r], preferred_element_type=F32
        )
        scores = scores[:n_rows] + scores[n_rows : 2 * n_rows] + scores[2 * n_rows :]
        exact_of.append(
            jnp.concatenate(
                [
                    scores[s * HEADS : (s + 1) * HEADS] + bias[s * REQ + r : s * REQ + r + 1, :]
                    for s in range(STEPS)
                ],
                axis=0,
            )
        )
    soft_of = []
    for exact in exact_of:
        top = jnp.max(exact, axis=1, keepdims=True)
        probs = jnp.exp(exact - top)
        soft_of.append((top, probs.astype(BF16), jnp.sum(probs, axis=1, keepdims=True)))
    for r, (top, probs, mass) in enumerate(soft_of):
        acc = jnp.dot(probs, vals_v[r], preferred_element_type=F32) / mass
        lse = top + jnp.log(mass)
        for s in range(STEPS):
            i = s * REQ + r
            rows = slice(s * HEADS, (s + 1) * HEADS)
            o_wide[pl.ds(i, HEADS, stride=SLOT), :] = acc[rows]
            stat = jnp.where(lane16 == i, lse[rows], stat)
    for i, piece in enumerate(split3(stat)):
        o_wide[pl.ds(STAT + i, HEADS, stride=SLOT), :] = piece.astype(F32)
    o_wide[pl.ds(SLOT - 1, HEADS, stride=SLOT), :] = jnp.zeros((HEADS, HD), F32)
    o_part[...] = o_wide[: HEADS * SLOT].astype(BF16)

    scatter(o_part, o_rs, slot, s_sem.at[3], (r_sem.at[5], r_sem.at[6]))
    copies = (iota((HD, HD), 0) == lax.rem(iota((HD, HD), 1), RANK)).astype(F32).astype(BF16)
    for r in range(REQ):
        low_keys[r // 2, :, (r % 2) * HD : (r % 2 + 1) * HD] = jnp.dot(
            keys_v[r], copies, preferred_element_type=F32
        ).astype(BF16)
    lane48 = iota((n_rows, HD), 1)
    for pair in range(REQ // 2):
        sides = []
        for half in range(2):
            hi, mid, lo = (p.astype(F32) for p in parts_of[2 * pair + half])
            packed = jnp.where(
                lane48 < RANK,
                hi,
                jnp.where(
                    lane48 < 2 * RANK,
                    pltpu.roll(mid, RANK, 1),
                    jnp.where(lane48 < 3 * RANK, pltpu.roll(lo, 2 * RANK, 1), 0.0),
                ),
            )
            blank = jnp.zeros((HD // 2, HD), F32)
            packed = jnp.concatenate([packed, blank[: HD // 2 - n_rows]], axis=0)
            sides.append(jnp.concatenate([blank, packed] if half else [packed, blank], axis=0).T)
        columns = jnp.concatenate(sides, axis=0).astype(BF16)
        rows = []
        for blk in range(n_local):
            part = jnp.dot(
                low_keys[pair, blk * BLK : (blk + 1) * BLK], columns, preferred_element_type=F32
            )
            peak = jnp.max(part, axis=0, keepdims=True)
            rows.append(peak + jnp.log(jnp.sum(jnp.exp(part - peak), axis=0, keepdims=True)))
        blocks = jnp.concatenate(rows, axis=0)
        lse_all[pair, :n_local] = blocks
        peak = jnp.max(blocks, axis=0, keepdims=True)
        low_own[0, pair : pair + 1] = peak + jnp.log(
            jnp.sum(jnp.exp(blocks - peak), axis=0, keepdims=True)
        )
    low_ring(0, dev_a)
    row16 = iota((SLOT, 1), 0)
    fresh = [
        jnp.where(
            row16 >= t * REQ,
            jnp.sum(q_mine * nk_rows[slot(t)], axis=1, keepdims=True),
            NONE,
        )
        for t in range(STEPS)
    ]
    top = jnp.maximum(jnp.maximum(fresh[0], fresh[1]), fresh[2])
    new_w = [jnp.exp(f - top) for f in fresh]
    new_sum = new_w[0] + new_w[1] + new_w[2]
    new_o = sum(
        new_w[t].astype(BF16).astype(F32) * nv_rows[slot(t)] for t in range(STEPS)
    ) / new_sum
    diag = iota((SLOT, HD), 0) == iota((SLOT, HD), 1)
    new_row = jnp.sum(jnp.where(diag, top + jnp.log(new_sum), 0.0), axis=0, keepdims=True)
    new_row = jnp.where(iota((1, HD), 1) < ROWS, new_row, NONE)

    outs = [o_wide[slot(mine)]]
    take(o_rs, len(NEAR) * SLOT, r_sem.at[5])
    for k in NEAR:
        outs.append(o_rs[slot(k)].astype(F32))
    res, row = merge(outs, [stat_of(p) for p in outs])
    outs = []
    take(o_rs, len(FAR) * SLOT, r_sem.at[6])
    for k in FAR:
        outs.append(o_rs[slot(k)].astype(F32))
    res, row = merge([res] + outs, [row] + [stat_of(p) for p in outs])
    o_own[...] = with_stat(res, row)
    exchange(o_own, o_ex, slot, s_sem.at[4], (r_sem.at[7], r_sem.at[8]))
    wo_t[...] = wo_v[...].astype(F32).T.astype(BF16)
    low_join(0, 7)
    low_ring(1, dev_b)
    outs = []
    take(o_ex, len(NEAR_RING) * SLOT, r_sem.at[7])
    for k in NEAR_RING:
        outs.append(o_ex[slot(k)].astype(F32))
    res, row = merge([res, new_o] + outs, [row, new_row] + [stat_of(p) for p in outs])
    outs = []
    take(o_ex, len(FAR_RING) * SLOT, r_sem.at[8])
    for k in FAR_RING:
        outs.append(o_ex[slot(k)].astype(F32))
    res, row = merge([res] + outs, [row] + [stat_of(p) for p in outs])
    o_all[slot(mine)] = jnp.where(iota((SLOT, HD), 0) < ROWS, res, 0.0).astype(BF16)
    gather(o_all, slot, s_sem.at[5], r_sem.at[9])
    low_join(1, 7)
    send(low_own.at[2], low_in.at[14], s_sem.at[7], r_sem.at[13], cross_a(0))
    take(o_all, 15 * SLOT, r_sem.at[9])

    terms = []
    for g in range(0, HEADS, 4):
        attn = jnp.concatenate([o_all[slot(h)] for h in range(g, g + 4)], axis=1)
        terms.append(
            jnp.dot(attn, wo_t[g * HD : (g + 4) * HD, :], preferred_element_type=F32)
        )
    term = ((terms[0] + terms[1]) + (terms[2] + terms[3])).astype(BF16)
    cols = term.shape[1]
    x_own[:, :cols] = term
    for k in (2, 1, 3):
        send(x_own, x_in.at[slot(k - 1)], s_sem.at[6], r_sem.at[10], dev_x(k))
    low_join(2, 1)
    for r in range(REQ):
        pair = r // 2
        mass = lse_all[pair] - low_own[3, pair : pair + 1]
        for s in range(STEPS):
            at_lane = (r % 2) * (HD // 2) + s * HEADS
            moved = pltpu.roll(mass, HD - at_lane, 1) if at_lane else mass
            mass_o[s, :, r, :] = moved[:n_local, :HEADS]
    take(x_in, 3 * SLOT, r_sem.at[10])
    term = term.astype(F32)
    for k in range(1, 4):
        term = term + x_in[slot(k - 1), :cols].astype(F32)
    for s in range(STEPS):
        out_o[s] = term[s * REQ : (s + 1) * REQ].astype(BF16)
    for i, (ref, rows) in enumerate(
        (
            (q_rs, 15 * ROWS), (q_ex, 7 * ROWS), (q_all, 15 * ROWS), (o_rs, 15 * SLOT),
            (o_ex, 7 * SLOT), (o_all, 15 * SLOT), (x_in, 3 * SLOT), (low_in, 15),
        )
    ):
        take(ref, rows, s_sem.at[i])


def hand_on(mass_i, out_i, mass_o, out_o, sem):
    copies = [
        pltpu.make_async_copy(mass_i, mass_o, sem.at[0]),
        pltpu.make_async_copy(out_i, out_o, sem.at[1]),
    ]
    for one in copies:
        one.start()
    for one in copies:
        one.wait()


def body(hidden, w_query, q_gain, basis, keys, values, new_keys, new_values, block_lists, w_out):
    n_tok = keys.shape[2]
    n_local = n_tok // BLK
    new_keys, new_values = new_keys[:, :, 0], new_values[:, :, 0]
    ops = (hidden, w_query, q_gain, basis, keys, values, new_keys, new_values, block_lists, w_out.T)
    ops = tuple(pltpu.with_memory_space_constraint(o, pltpu.HBM) for o in ops)
    slots = lambda n, kind=F32: pltpu.VMEM((n * SLOT, HD), kind)
    landing = [pltpu.VMEM(o.shape, o.dtype) for o in ops]
    landing[4] = landing[5] = pltpu.VMEM((REQ, n_tok, HD), BF16)
    dma = lambda n: pltpu.SemaphoreType.DMA((n,))

    def run(*refs):
        refs = list(refs)
        refs[4] = refs[4].at[:, 0]
        refs[5] = refs[5].at[:, 0]
        kernel(*refs)

    shapes = (
        jax.ShapeDtypeStruct((STEPS, n_local, REQ, HEADS), F32),
        jax.ShapeDtypeStruct((STEPS, REQ, w_out.shape[1]), BF16),
    )
    raw = pl.pallas_call(
        run,
        out_shape=shapes,
        in_specs=[pl.BlockSpec(memory_space=pl.ANY)] * len(ops),
        out_specs=(pl.BlockSpec(memory_space=pltpu.VMEM),) * 2,
        scratch_shapes=landing
        + [
            pltpu.VMEM((SLOT, block_lists.shape[3]), jnp.int32),
            pltpu.VMEM((SLOT, n_tok), F32),
            slots(STEPS),
            slots(STEPS),
            pltpu.VMEM((6 * HD, HD), BF16),
            pltpu.VMEM((w_out.shape[0], w_out.shape[1]), BF16),
            pltpu.VMEM((REQ, HD, n_tok), BF16),
            pltpu.VMEM((REQ // 2, n_tok, 2 * HD), BF16),
        ]
        + [slots(n) for n in (16, 15, 1, 7, 17, 17)]
        + [pltpu.VMEM((REQ // 2, SLOT, HD), F32)]
        + [slots(n, BF16) for n in (16, 15, 1, 7, 16, 1, 3)]
        + [pltpu.VMEM((n, REQ // 2, HD), F32) for n in (4, 15)]
        + [dma(n) for n in (10, 8, 14)],
        compiler_params=pltpu.CompilerParams(
            collective_id=0, has_side_effects=True, vmem_limit_bytes=32 * 2**20
        ),
        name="decode",
    )(*ops)
    mass, layer_out = pl.pallas_call(
        hand_on,
        out_shape=shapes,
        in_specs=[pl.BlockSpec(memory_space=pl.ANY)] * 2,
        out_specs=(pl.BlockSpec(memory_space=pl.ANY),) * 2,
        scratch_shapes=[dma(2)],
        compiler_params=pltpu.CompilerParams(vmem_limit_bytes=32 * 2**20),
        name="hand_on",
    )(*raw)
    return mass.transpose(0, 2, 3, 1), layer_out


def solution(mesh):
    placed = (
        P(None, None, "ctx"),
        P("ctx", "kvh"),
        P(),
        P("kvh", None, None),
        P(None, "kvh", "ctx", None),
        P(None, "kvh", "ctx", None),
        P(None, None, "kvh", None),
        P(None, None, "kvh", None),
        P(None, None, "kvh", None),
        P("kvh", "ctx"),
    )
    return jax.shard_map(
        body,
        mesh=mesh,
        in_specs=placed,
        out_specs=(P(None, None, "kvh", "ctx"), P(None, None, "ctx")),
        check_vma=False,
    )
```
